32 devices in a mesh: seq: 4 (over y, x), expert: 8 (over z, core).
Axes of the slice: x: 2, y: 2, z: 4, core: 2. Of those that a mesh axis runs over, the one named last changes fastest.
Arguments:
- query_rows: bfloat16 [8, 512, 2048], P('expert', 'seq'), may hold values from -2000 to 2000
- key_rows: bfloat16 [8, 512, 2048], P('expert', 'seq'), may hold values from -4 to 4
- value_rows: bfloat16 [8, 512, 2048], P('expert', 'seq'), may hold values from -48 to 48
- norm_gain: float32 [2048], replicated, may hold values from 0.1 to 1.9
- expert_ids: int32 [8, 512, 2], P('expert', 'seq'), may hold values from 0 to 7, all different within a row; in each aligned block of 128 rows (0 to 127, 128 to 255, ..., all dimensions but the last counted through in order) at most 32 rows name the same one
- gate_weights: float32 [8, 512, 2], P('expert', 'seq'), may hold values from 0.1 to 1
- w_gate: bfloat16 [8, 2048, 768], P('expert'), may hold values from -0.125 to 0.125
- w_up: bfloat16 [8, 2048, 768], P('expert'), may hold values from -0.125 to 0.125
- w_down: bfloat16 [8, 768, 2048], P('expert'), may hold values from -0.21875 to 0.21875
Outputs:
- layer_out: bfloat16 [8, 512, 2048], P('expert', 'seq')
The draws below stay inside these ranges and needn't reach their ends.
Inputs may be any that keep to these rules, and one draw needn't show every extreme that they name: `expert_ids`: within the tokens of one device (aligned blocks of 128 tokens of a sequence) no expert is named by more than 32 choices, a bound that some block reaches; a token's two ids differ.
All inputs are finite; a program needn't handle non-finite values.
Results may differ from the reference program's by a relative error of at most 0.017.
Values may be sent and summed in bfloat16 or wider, within the bound.
No kernel may reach another device: no remote copies, remote signals or barrier semaphores. Data moves between devices by JAX's collectives and lax.ppermute only.
A program may use at most 128 MiB of HBM per device.

```python
import math
import jax
import jax.numpy as jnp
import numpy as np
from jax import lax

D = 2048
HEADS = 16
DH = 128
FF = 768
TOK_DEV = 128
LENGTH = 512
SEQS = 8
EXPERTS = 8
CAP = 32
N_SEQ = 4
N_EXPERT = 8


def key_field_draw(key):
    field = jax.random.truncated_normal(jax.random.fold_in(key, 11), -4.0, 4.0, (SEQS, LENGTH, HEADS, DH), jnp.float32)
    return field


def draw_key_rows(key, part):
    field = key_field_draw(key)
    return field.reshape(SEQS, LENGTH, D).astype(jnp.bfloat16)


def draw_query_rows(key, part):
    base = jax.random.truncated_normal(jax.random.fold_in(key, 21), -4.0, 4.0, (SEQS, LENGTH, HEADS, DH), jnp.float32)
    return base.reshape(SEQS, LENGTH, D).astype(jnp.bfloat16)


def block_scale(stream_key, dims, split, smallest, high):
    gain = 1.0
    for dim, blocks in split:
        draws = jax.random.uniform(jax.random.fold_in(jax.random.fold_in(stream_key, 6), dim), (blocks,), jnp.float32, smallest / len(split), high / len(split))
        gain = gain * jnp.repeat(jnp.exp(draws), dims[dim] // blocks).reshape((-1,) + (1,) * (len(dims) - 1 - dim))
    return gain


def routed_block(own_key, own, number, rows, number_of, top, most, slope):
    sequence = jax.random.permutation(own_key, number_of)
    heavy_load, ordinary = portions_of(number_of, rows * top, most, slope, True), portions_of(number_of, rows * top, most, slope, False)
    places = jnp.arange(number_of)

    def named(sizes, rotation):
        used = int((sizes > 0).sum())
        fixed = max(1, used // 4)
        shifted = fixed + (places - fixed + rotation * (used - fixed)) % max(1, number_of - fixed)
        return jnp.zeros((number_of,), jnp.int32).at[sequence[jnp.where(places < fixed, places, shifted)]].set(jnp.asarray(sizes, jnp.int32))

    sizes = jnp.where(number % 4 == 0, named(heavy_load, number // 4), named(ordinary, number - number // 4 - 1))
    mixed = jax.random.permutation(jax.random.fold_in(own, 3), number_of)
    donor, sink = mixed[0:number_of // 2 * 2:2], mixed[1:number_of // 2 * 2:2]
    slack = jnp.minimum(sizes[donor] - 1, most - sizes[sink]) // 2
    slack = jnp.where((donor == sequence[0]) | (sink == sequence[0]) | (sizes[sink] == 0), 0, jnp.maximum(slack, 0))
    shifted = jax.random.randint(jax.random.fold_in(own, 4), (number_of // 2,), 0, 1 << 20) % (slack + 1)
    sizes = sizes.at[donor].add(-shifted).at[sink].add(shifted)
    items = jnp.searchsorted(jnp.cumsum(sizes), jnp.arange(rows * top), side="right").astype(jnp.int32)
    listing = items.reshape(top, rows).T
    listing = listing[jax.random.permutation(jax.random.fold_in(own, 1), rows)]
    rotation = jax.random.randint(jax.random.fold_in(own, 2), (rows, 1), 0, top)
    return jnp.take_along_axis(listing, (jnp.arange(top)[None, :] + rotation) % top, axis=1)


def portions_of(number_of, total, reach, lean, full):
    loads = [(1 << 20) // math.isqrt(rank ** lean) + 1 for rank in range(1, number_of + 1)]
    largest = reach if full else min(reach, max(-(-total // number_of), total * loads[0] // sum(loads)))
    least = 1 if total - largest >= number_of - 1 else 0
    counts, rest = [largest] + [least] * (number_of - 1), total - largest - least * (number_of - 1)
    while rest > 0:
        candidates = [i for i in range(1, number_of) if counts[i] < largest] or [i for i in range(1, number_of) if counts[i] < reach]
        mass, remaining = sum([loads[i] for i in candidates]), rest
        for i in candidates:
            more = min(reach - counts[i], max(1, remaining * loads[i] // mass), rest)
            counts[i] = counts[i] + more
            rest = rest - more
    return np.array(counts)


def noise(stream_key, dims, spread, limit, shards=(), held_as=jnp.bfloat16):
    drawn = spread * jax.random.normal(stream_key, dims, jnp.float32)
    if shards:
        drawn = drawn * block_scale(stream_key, dims, shards, -0.22, 0.18)
    return jnp.clip(drawn, -limit, limit).astype(held_as)


def setup_inputs(seed: int = 0) -> dict:
    splits = jax.random.split(jax.random.key(seed), 10)
    query_rows = draw_query_rows(jax.random.fold_in(splits[9], 71), 0)
    key_rows = draw_key_rows(jax.random.fold_in(splits[9], 71), 0)
    value_rows = noise(splits[2], (SEQS, LENGTH, D), 8.0, 48.0, ((0, 8), (1, 4)))
    norm_gain = jnp.clip(1.0 + 0.18 * jax.random.normal(splits[3], (D,), jnp.float32), 0.1, 1.9)
    expert_ids_keys = jax.random.split(jax.random.fold_in(splits[4], 1), SEQS * LENGTH // TOK_DEV)
    expert_ids_turns = jax.random.permutation(jax.random.fold_in(splits[4], 3), SEQS * LENGTH // TOK_DEV)
    expert_ids = jax.vmap(lambda own, number: routed_block(jax.random.fold_in(splits[4], 2), own, number, TOK_DEV, EXPERTS, 2, CAP, 2))(expert_ids_keys, expert_ids_turns).reshape((SEQS, LENGTH, 2))
    gate_weights = jnp.clip(0.1 + 0.9 * jax.random.uniform(splits[5], (SEQS, LENGTH, 2), jnp.float32) ** block_scale(splits[5], (SEQS, LENGTH, 2), ((0, 8), (1, 4)), -0.2, 0.2), 0.1, 1.0)
    w_gate = noise(splits[6], (EXPERTS, D, FF), D ** -0.5, 0.125, ((0, 8),))
    w_up = noise(splits[7], (EXPERTS, D, FF), D ** -0.5, 0.125, ((0, 8),))
    w_down = noise(splits[8], (EXPERTS, FF, D), FF ** -0.5, 0.21875, ((0, 8),))
    return {"query_rows": query_rows, "key_rows": key_rows, "value_rows": value_rows, "norm_gain": norm_gain, "expert_ids": expert_ids, "gate_weights": gate_weights, "w_gate": w_gate, "w_up": w_up, "w_down": w_down}


def head_attention(operands):
    query_head, key_head, value_head = operands
    scores = jnp.dot(query_head, key_head.T, preferred_element_type=jnp.float32) * DH ** (-0.5)
    row_peak = lax.optimization_barrier(jnp.max(scores, axis=-1, keepdims=True))
    exponentials = jnp.exp(scores - row_peak)
    totals = lax.optimization_barrier(jnp.sum(exponentials, axis=-1, keepdims=True))
    weighted = jnp.dot(exponentials.astype(jnp.bfloat16), value_head, preferred_element_type=jnp.float32)
    return (weighted / totals).astype(jnp.bfloat16)

def split_heads(block):
    return block.reshape(LENGTH, HEADS, DH).transpose(1, 0, 2)

def sequence_attention(operands):
    query_seq, key_seq, value_seq = operands
    result = lax.map(head_attention, (split_heads(query_seq), split_heads(key_seq), split_heads(value_seq)))
    return result.transpose(1, 0, 2).reshape(LENGTH, D)

def reference(query_rows, key_rows, value_rows, norm_gain, expert_ids, gate_weights, w_gate, w_up, w_down):
    attended = lax.map(sequence_attention, (query_rows, key_rows, value_rows))
    widened = attended.reshape(SEQS * LENGTH, D).astype(jnp.float32)
    normed = (widened * lax.rsqrt(lax.optimization_barrier(jnp.mean(widened * widened, axis=-1, keepdims=True)) + 1e-06) * norm_gain.astype(jnp.float32)).astype(jnp.bfloat16)
    choice_ids = expert_ids.reshape(-1).astype(jnp.int32)
    choice_gates = gate_weights.reshape(-1)
    owners = (jnp.arange(choice_ids.shape[0]) // 2).astype(jnp.int32)
    room_size = N_SEQ * N_EXPERT * CAP

    def one_expert(summed, operands):
        expert, gate_mat, up_mat, down_mat = operands
        matches = choice_ids == expert
        picked = jnp.nonzero(matches, size=room_size, fill_value=0)[0].astype(jnp.int32)
        live_count = jnp.minimum(jnp.sum(matches.astype(jnp.int32)), room_size)
        live_mask = (jnp.arange(room_size) < live_count).astype(jnp.float32)
        inputs = normed[owners[picked]]
        gate_part = jnp.dot(inputs, gate_mat, preferred_element_type=jnp.float32)
        up_part = jnp.dot(inputs, up_mat, preferred_element_type=jnp.float32)
        hidden = (jax.nn.silu(gate_part) * up_part).astype(jnp.bfloat16)
        produced = jnp.dot(hidden, down_mat, preferred_element_type=jnp.float32).astype(jnp.bfloat16)
        factor = choice_gates[picked].astype(jnp.float32) * live_mask
        summed = summed.at[owners[picked]].add(factor[:, None] * produced.astype(jnp.float32))
        return (summed, None)
    start_sum = jnp.zeros((SEQS * LENGTH, D), jnp.float32)
    summed, unused = lax.scan(one_expert, start_sum, (jnp.arange(EXPERTS).astype(jnp.int32), w_gate, w_up, w_down))
    mixture = (widened + summed).astype(jnp.bfloat16)
    return mixture.reshape(SEQS, LENGTH, D)
```

```python
import functools

import jax
import jax.numpy as jnp
from jax import lax
from jax.experimental import pallas as pl
from jax.experimental.pallas import tpu as pltpu
from jax.sharding import PartitionSpec as P

HEADS = 16
CAP = 32
CHUNKS = 1
F32 = jnp.float32
BF16 = jnp.bfloat16
ANY = pl.BlockSpec(memory_space=pl.ANY)
VMEM = pl.BlockSpec(memory_space=pltpu.VMEM)


def swap(x, axis, distance):
    size = lax.axis_size(axis)
    return lax.ppermute(x, axis, [(i, i ^ distance) for i in range(size)])


def params(mib):
    return pltpu.CompilerParams(vmem_limit_bytes=mib << 20)


def cost(flops, moved):
    return pl.CostEstimate(flops=flops, bytes_accessed=moved, transcendentals=0)


def pack_kernel(groups, group_width, start, width, q_ref, k_ref, v_ref, *rest):
    outs, sems = rest[:-1], rest[-1]
    me = lax.axis_index("seq")
    copies = []
    for distance in range(1, groups):
        column = pl.multiple_of((me ^ distance) * group_width + start, 128)
        for i, ref in enumerate((q_ref, k_ref, v_ref)):
            copies.append(
                pltpu.make_async_copy(
                    ref.at[0, :, pl.ds(column, width)],
                    outs[distance - 1].at[i],
                    sems.at[3 * (distance - 1) + i],
                )
            )
    for copy in copies:
        copy.start()
    for copy in copies:
        copy.wait()


def pack(groups, group_width, start, width, q, k, v):
    tokens = q.shape[1]
    return pl.pallas_call(
        functools.partial(pack_kernel, groups, group_width, start, width),
        out_shape=[jax.ShapeDtypeStruct((3, tokens, width), BF16)] * (groups - 1),
        in_specs=[ANY] * 3,
        out_specs=[ANY] * (groups - 1),
        scratch_shapes=[pltpu.SemaphoreType.DMA((3 * (groups - 1),))],
        compiler_params=params(8),
        cost_estimate=cost(0, 2 * 3 * (groups - 1) * tokens * width * 2),
        name="pack_heads",
    )(q, k, v)


def attend_kernel(groups, group_width, start, width, head_size, q_ref, k_ref, v_ref, *rest):
    received, outs = rest[: groups - 1], rest[groups - 1 : 2 * groups - 1]
    q_all, k_all, v_all, sems = rest[2 * groups - 1 :]
    tokens = outs[0].shape[0]
    me = lax.axis_index("seq")
    column = pl.multiple_of(me * group_width + start, 128)
    copies = []
    for i, (ref, held) in enumerate(((q_ref, q_all), (k_ref, k_all), (v_ref, v_all))):
        copies.append(
            pltpu.make_async_copy(
                ref.at[0, :, pl.ds(column, width)], held.at[pl.ds(0, tokens)], sems.at[i]
            )
        )
        for j in range(groups - 1):
            copies.append(
                pltpu.make_async_copy(
                    received[j].at[i],
                    held.at[pl.ds((j + 1) * tokens, tokens)],
                    sems.at[3 * (j + 1) + i],
                )
            )
    for copy in copies:
        copy.start()
    for copy in copies:
        copy.wait()
    for head in range(width // head_size):
        lanes = slice(head * head_size, (head + 1) * head_size)
        keys, values = k_all[:, lanes], v_all[:, lanes]
        for block in range(groups):
            rows = slice(block * tokens, (block + 1) * tokens)
            scores = lax.dot_general(
                q_all[rows, lanes], keys, (((1,), (1,)), ((), ())), preferred_element_type=F32
            ) * (head_size**-0.5)
            peak = jnp.max(scores, axis=-1, keepdims=True)
            exponentials = jnp.exp(scores - peak)
            totals = jnp.sum(exponentials, axis=-1, keepdims=True)
            weighted = jnp.dot(exponentials.astype(BF16), values, preferred_element_type=F32)
            outs[block][:, lanes] = (weighted / totals).astype(BF16)


def attend(groups, group_width, start, width, head_size, q, k, v, received):
    tokens = q.shape[1]
    total = groups * tokens
    return pl.pallas_call(
        functools.partial(attend_kernel, groups, group_width, start, width, head_size),
        out_shape=[jax.ShapeDtypeStruct((tokens, width), BF16)] * groups,
        in_specs=[ANY] * (3 + groups - 1),
        out_specs=[VMEM] * groups,
        scratch_shapes=[pltpu.VMEM((total, width), BF16)] * 3
        + [pltpu.SemaphoreType.DMA((3 * groups,))],
        compiler_params=params(32),
        cost_estimate=cost(16 * total * total * width, 8 * total * width),
        name="attend",
    )(q, k, v, *received)


def slot_matrix(experts, ids):
    tokens = ids.shape[1]
    me = lax.axis_index("expert")
    named = lax.broadcasted_iota(jnp.int32, (experts, tokens), 0) ^ me
    matches = jnp.where((ids[0:1, :] == named) | (ids[1:2, :] == named), 1.0, 0.0)
    earlier = jnp.where(
        lax.broadcasted_iota(jnp.int32, (tokens, tokens), 0)
        < lax.broadcasted_iota(jnp.int32, (tokens, tokens), 1),
        1.0,
        0.0,
    )
    rank = jnp.dot(matches.astype(BF16), earlier.astype(BF16), preferred_element_type=F32)
    rank = jnp.where(matches > 0.0, rank, -1.0).astype(jnp.int32)
    slots = lax.broadcasted_iota(jnp.int32, (CAP, tokens), 0)
    return [slots == rank[d : d + 1, :] for d in range(experts)], named


def select_kernel(groups, experts, width, ids_ref, *rest):
    blocks, outs = rest[:groups], rest[groups : groups + experts]
    kept, sems = rest[groups + experts :]
    me = lax.axis_index("seq")
    copies = []
    for d in range(groups):
        column = pl.multiple_of((me ^ d) * width, 128)
        copies.append(
            pltpu.make_async_copy(blocks[d], kept.at[:, pl.ds(column, width)], sems.at[d])
        )
    for copy in copies:
        copy.start()
    hits, _ = slot_matrix(experts, ids_ref[...])
    chosen = jnp.concatenate([jnp.where(h, 1.0, 0.0).astype(BF16) for h in hits], axis=0)
    for copy in copies:
        copy.wait()
    picked = jnp.dot(chosen, kept[...], preferred_element_type=F32).astype(BF16)
    for d in range(experts):
        outs[d][...] = picked[d * CAP : (d + 1) * CAP]


def select(groups, experts, ids, blocks):
    tokens, width = blocks[0].shape
    full = groups * width
    return pl.pallas_call(
        functools.partial(select_kernel, groups, experts, width),
        out_shape=[jax.ShapeDtypeStruct((CAP, full), BF16)] * experts
        + [jax.ShapeDtypeStruct((tokens, full), BF16)],
        in_specs=[VMEM] + [ANY] * groups,
        out_specs=[VMEM] * (experts + 1),
        scratch_shapes=[pltpu.SemaphoreType.DMA((groups,))],
        compiler_params=params(16),
        cost_estimate=cost(2 * experts * CAP * tokens * full, 8 * tokens * full),
        name="select_rows",
    )(ids, *blocks)


def experts_kernel(groups, count, widths, gain_ref, gate_ref, up_ref, down_ref, *rest):
    chunks = len(widths)
    blocks, outs = rest[: count * chunks], rest[count * chunks : count * chunks + count]
    rows_ref, total_ref = rest[count * chunks + count :]
    step = pl.program_id(0)

    @pl.when(step == 0)
    def _():
        stride = sum(widths)
        for i in range(count):
            parts = []
            for g in range(groups):
                for c, w in enumerate(widths):
                    parts.append(blocks[i * chunks + c][:, g * w : (g + 1) * w].astype(F32))
            row = jnp.concatenate(parts, axis=1) if len(parts) > 1 else parts[0]
            scale = lax.rsqrt(jnp.mean(row * row, axis=-1, keepdims=True) + 1e-06)
            rows_ref[i * CAP : (i + 1) * CAP, :] = (row * scale * gain_ref[...]).astype(BF16)
        del stride

    rows = rows_ref[...]
    gate = jnp.dot(rows, gate_ref[0], preferred_element_type=F32)
    up = jnp.dot(rows, up_ref[0], preferred_element_type=F32)
    hidden = (gate / (1.0 + jnp.exp(-gate)) * up).astype(BF16)
    part = jnp.dot(hidden, down_ref[0], preferred_element_type=F32)

    @pl.when(step == 0)
    def _():
        total_ref[...] = part

    @pl.when(step > 0)
    def _():
        total_ref[...] += part

    @pl.when(step == pl.num_programs(0) - 1)
    def _():
        for i in range(count):
            outs[i][...] = total_ref[i * CAP : (i + 1) * CAP, :].astype(BF16)


def run_experts(groups, widths, gain, w_gate, w_up, w_down, blocks):
    count = len(blocks)
    features, units = w_gate.shape[1:]
    tile = 256 if units % 256 == 0 else 128
    flat = [part for block in blocks for part in block]
    return pl.pallas_call(
        functools.partial(experts_kernel, groups, count, widths),
        grid=(units // tile,),
        out_shape=[jax.ShapeDtypeStruct((CAP, features), BF16)] * count,
        in_specs=[
            pl.BlockSpec((1, features), lambda i: (0, 0)),
            pl.BlockSpec((1, features, tile), lambda i: (0, 0, i)),
            pl.BlockSpec((1, features, tile), lambda i: (0, 0, i)),
            pl.BlockSpec((1, tile, features), lambda i: (0, i, 0)),
        ]
        + [pl.BlockSpec(part.shape, lambda i: (0, 0)) for part in flat],
        out_specs=[pl.BlockSpec((CAP, features), lambda i: (0, 0))] * count,
        scratch_shapes=[
            pltpu.VMEM((count * CAP, features), BF16),
            pltpu.VMEM((count * CAP, features), F32),
        ],
        compiler_params=params(32),
        cost_estimate=cost(6 * count * CAP * features * units, 6 * features * units),
        name="experts",
    )(gain, w_gate, w_up, w_down, *flat)


def combine_kernel(groups, experts, widths, ids_ref, gates_ref, *rest):
    chunks = len(widths)
    kept, blocks, out_ref = rest[:chunks], rest[chunks : chunks + experts], rest[-1]
    ids, gates = ids_ref[...], gates_ref[...]
    hits, named = slot_matrix(experts, ids)
    weight = jnp.where(ids[0:1, :] == named, gates[0:1, :], 0.0) + jnp.where(
        ids[1:2, :] == named, gates[1:2, :], 0.0
    )
    coarse = weight.astype(BF16).astype(F32)
    fine = weight - coarse
    spread = []
    for part in (coarse, fine):
        for d in range(experts):
            spread.append(jnp.where(hits[d], part[d : d + 1, :], 0.0).astype(BF16))
    spread = jnp.concatenate(spread, axis=0)
    rows = jnp.concatenate([block[...] for block in blocks], axis=0)
    mixture = lax.dot_general(
        spread,
        jnp.concatenate([rows, rows], axis=0),
        (((0,), (0,)), ((), ())),
        preferred_element_type=F32,
    )
    column = 0
    for g in range(groups):
        for c, w in enumerate(widths):
            part = kept[c][:, g * w : (g + 1) * w].astype(F32)
            out_ref[0, :, column : column + w] = (part + mixture[:, column : column + w]).astype(
                BF16
            )
            column += w


def combine(groups, widths, ids, gates, kept, blocks):
    tokens, features = ids.shape[1], blocks[0].shape[1]
    experts = len(blocks)
    return pl.pallas_call(
        functools.partial(combine_kernel, groups, experts, widths),
        out_shape=jax.ShapeDtypeStruct((1, tokens, features), BF16),
        in_specs=[VMEM] * (2 + len(widths) + experts),
        out_specs=VMEM,
        compiler_params=params(32),
        cost_estimate=cost(4 * experts * CAP * tokens * features, 8 * tokens * features),
        name="combine",
    )(ids, gates, *kept, *blocks)


def local(
    query_rows, key_rows, value_rows, norm_gain, expert_ids, gate_weights, w_gate, w_up, w_down
):
    features = query_rows.shape[2]
    head_size = features // HEADS
    groups, experts = lax.axis_size("seq"), lax.axis_size("expert")
    per_group = HEADS // groups
    group_width = per_group * head_size
    chunks = CHUNKS if per_group % CHUNKS == 0 else 1
    width = group_width // chunks
    widths = (width,) * chunks
    ids, gates = expert_ids[0].T, gate_weights[0].T
    gain = norm_gain.reshape(1, features)

    received = []
    for c in range(chunks):
        packed = pack(groups, group_width, c * width, width, query_rows, key_rows, value_rows)
        received.append([swap(packed[d - 1], "seq", d) for d in range(1, groups)])
    kept, arrived = [], []
    for c in range(chunks):
        heads = attend(
            groups, group_width, c * width, width, head_size,
            query_rows, key_rows, value_rows, received[c],
        )
        blocks = [heads[0]] + [swap(heads[d], "seq", d) for d in range(1, groups)]
        *rows, own = select(groups, experts, ids, blocks)
        kept.append(own)
        arrived.append([rows[0]] + [None] * (experts - 1))
        for d in list(range(experts // 2, experts)) + list(range(1, experts // 2)):
            arrived[c][d] = swap(rows[d], "expert", d)
    half, quarter = experts // 2, experts // 4
    returned = [None] * experts
    for members in (
        range(half, half + quarter),
        range(half + quarter, experts),
        range(half),
    ):
        produced = run_experts(
            groups, widths, gain, w_gate, w_up, w_down,
            [[arrived[c][d] for c in range(chunks)] for d in members],
        )
        for d, block in zip(members, produced):
            returned[d] = block if d == 0 else swap(block, "expert", d)
    return combine(groups, widths, ids, gates, kept, returned)


def solution(mesh):
    rows = P("expert", "seq", None)
    weights = P("expert", None, None)
    return jax.shard_map(
        local,
        mesh=mesh,
        in_specs=(rows, rows, rows, P(), rows, rows, weights, weights, weights),
        out_specs=rows,
        check_vma=False,
    )
```

```python
import functools
import math

import jax
import jax.numpy as jnp
from jax import lax
from jax.experimental import pallas as pl
from jax.experimental.pallas import tpu as pltpu
from jax.sharding import PartitionSpec as P

HEADS = 16
CAP = 32
CHUNKS = 2
PACK_MIB = 56
F32 = jnp.float32
BF16 = jnp.bfloat16
HBM = pl.BlockSpec(memory_space=pltpu.HBM)
VMEM = pl.BlockSpec(memory_space=pltpu.VMEM)


def swap(x, axis, distance):
    size = lax.axis_size(axis)
    return lax.ppermute(x, axis, [(i, i ^ distance) for i in range(size)])


def params(mib):
    return pltpu.CompilerParams(vmem_limit_bytes=mib << 20)


def cost(flops, moved):
    return pl.CostEstimate(flops=flops, bytes_accessed=moved, transcendentals=0)


def pack_kernel(groups, chunks, c, width, q_ref, k_ref, v_ref, *rest):
    outs, sems = rest[:-1], rest[-1]
    me = lax.axis_index("seq")
    copies = []
    for distance in range(groups):
        column = pl.multiple_of(((me ^ distance) * chunks + c) * width, 128)
        for i, ref in enumerate((q_ref, k_ref, v_ref)):
            copies.append(
                pltpu.make_async_copy(
                    ref.at[0, :, pl.ds(column, width)], outs[distance].at[i], sems.at[len(copies)]
                )
            )
    for copy in copies:
        copy.start()
    for copy in copies:
        copy.wait()


def pack(groups, chunks, c, width, q, k, v):
    tokens = q.shape[1]
    count = groups
    return pl.pallas_call(
        functools.partial(pack_kernel, groups, chunks, c, width),
        out_shape=[jax.ShapeDtypeStruct((3, tokens, width), BF16)] * count,
        in_specs=[HBM] * 3,
        out_specs=[VMEM] * count,
        scratch_shapes=[pltpu.SemaphoreType.DMA((3 * count,))],
        compiler_params=params(PACK_MIB if c == 0 else 8),
        cost_estimate=cost(0, 2 * 3 * count * tokens * width * 2),
        name="pack_heads",
    )(q, k, v)


def attend_kernel(groups, width, head_size, *rest):
    blocks, outs = rest[:groups], rest[groups : 2 * groups]
    q_all, k_all, v_all, sems = rest[2 * groups :]
    tokens = outs[0].shape[0]
    copies = []
    for i, held in enumerate((q_all, k_all, v_all)):
        for j in range(groups):
            copies.append(
                pltpu.make_async_copy(
                    blocks[j].at[i], held.at[pl.ds(j * tokens, tokens)], sems.at[len(copies)]
                )
            )
    for copy in copies:
        copy.start()
    for copy in copies:
        copy.wait()
    scale = head_size**-0.5 * math.log2(math.e)
    for head in range(width // head_size):
        lanes = slice(head * head_size, (head + 1) * head_size)
        keys, values = k_all[:, lanes], v_all[:, lanes]
        for block in range(groups):
            rows = slice(block * tokens, (block + 1) * tokens)
            scores = lax.dot_general(
                q_all[rows, lanes], keys, (((1,), (1,)), ((), ())), preferred_element_type=F32
            )
            peak = jnp.max(scores, axis=-1, keepdims=True)
            exponentials = jnp.exp2((scores - peak) * scale)
            totals = jnp.sum(exponentials, axis=-1, keepdims=True)
            weighted = jnp.dot(exponentials.astype(BF16), values, preferred_element_type=F32)
            outs[block][:, lanes] = (weighted / totals).astype(BF16)


def attend(width, head_size, blocks):
    groups, tokens = len(blocks), blocks[0].shape[1]
    total = groups * tokens
    return pl.pallas_call(
        functools.partial(attend_kernel, groups, width, head_size),
        out_shape=[jax.ShapeDtypeStruct((tokens, width), BF16)] * groups,
        in_specs=[HBM] * groups,
        out_specs=[VMEM] * groups,
        scratch_shapes=[pltpu.VMEM((total, width), BF16)] * 3
        + [pltpu.SemaphoreType.DMA((3 * groups,))],
        compiler_params=params(32),
        cost_estimate=cost(160 * total * total * width, 80 * total * width),
        name="attend",
    )(*blocks)


def slot_matrix(experts, ids):
    tokens = ids.shape[1]
    me = lax.axis_index("expert")
    named = lax.broadcasted_iota(jnp.int32, (experts, tokens), 0) ^ me
    matches = jnp.where((ids[0:1, :] == named) | (ids[1:2, :] == named), 1.0, 0.0)
    earlier = jnp.where(
        lax.broadcasted_iota(jnp.int32, (tokens, tokens), 0)
        < lax.broadcasted_iota(jnp.int32, (tokens, tokens), 1),
        1.0,
        0.0,
    )
    rank = jnp.dot(matches.astype(BF16), earlier.astype(BF16), preferred_element_type=F32)
    rank = jnp.where(matches > 0.0, rank, -1.0).astype(jnp.int32)
    slots = lax.broadcasted_iota(jnp.int32, (CAP, tokens), 0)
    return [slots == rank[d : d + 1, :] for d in range(experts)], named


def select_kernel(groups, experts, width, earlier, last, ids_ref, *rest):
    blocks, before = rest[:groups], rest[groups : groups + earlier]
    half, middle = experts // 2, experts // 2 + experts // 4
    count = experts if last else middle - half
    outs = rest[groups + earlier : groups + earlier + count]
    kept, sems = rest[groups + earlier + count :]
    me = lax.axis_index("seq")
    copies = []
    for d in range(groups):
        column = pl.multiple_of((me ^ d) * width, 128)
        copies.append(
            pltpu.make_async_copy(blocks[d], kept.at[:, pl.ds(column, width)], sems.at[d])
        )
    for copy in copies:
        copy.start()
    hits, _ = slot_matrix(experts, ids_ref[...])
    chosen = [jnp.where(h, 1.0, 0.0).astype(BF16) for h in hits]
    for copy in copies:
        copy.wait()

    def pick(distances, rows, first):
        picked = jnp.dot(
            jnp.concatenate([chosen[d] for d in distances], axis=0),
            rows,
            preferred_element_type=F32,
        ).astype(BF16)
        for i in range(len(distances)):
            outs[first + i][...] = picked[i * CAP : (i + 1) * CAP]

    pick(range(half, middle), kept[...], 0)
    if last:
        parts = [ref[...] for ref in before] + [kept[...]]
        full = jnp.concatenate(parts, axis=1) if earlier else parts[0]
        pick([*range(middle, experts), *range(half)], full, middle - half)


def select(groups, experts, ids, blocks, before, last):
    tokens, width = blocks[0].shape
    part = groups * width
    whole = part * (len(before) + 1)
    quarter = experts // 4
    shapes = [(CAP, part)] * quarter
    if last:
        shapes += [(CAP, whole)] * (experts - quarter)
    shapes.append((tokens, part))
    return pl.pallas_call(
        functools.partial(select_kernel, groups, experts, width, len(before), last),
        out_shape=[jax.ShapeDtypeStruct(shape, BF16) for shape in shapes],
        in_specs=[VMEM] + [HBM] * groups + [VMEM] * len(before),
        out_specs=[VMEM] * len(shapes),
        scratch_shapes=[pltpu.SemaphoreType.DMA((groups,))],
        compiler_params=params(16),
        cost_estimate=cost(2 * experts * CAP * tokens * part, 8 * tokens * part),
        name="select_rows",
    )(ids, *blocks, *before)


def experts_kernel(
    groups, chunks, width, count, held, gain_ref, gate_ref, up_ref, down_ref, *rest
):
    blocks, outs = rest[: count * held], rest[count * held : count * held + count]
    rows_ref, total_ref = rest[count * held + count :]
    step = pl.program_id(0)

    @pl.when(step == 0)
    def _():
        for i in range(count):
            mine = [blocks[k][...] for k in range(i * held, (i + 1) * held)]
            row = jnp.concatenate(mine, axis=1) if held > 1 else mine[0]
            parts = []
            for g in range(groups):
                for c in range(chunks):
                    first = (c * groups + g) * width
                    parts.append(row[:, first : first + width].astype(F32))
            row = jnp.concatenate(parts, axis=1)
            scale = lax.rsqrt(jnp.mean(row * row, axis=-1, keepdims=True) + 1e-06)
            rows_ref[i * CAP : (i + 1) * CAP, :] = (row * scale * gain_ref[...]).astype(BF16)

    rows = rows_ref[...]
    gate = jnp.dot(rows, gate_ref[0], preferred_element_type=F32)
    up = jnp.dot(rows, up_ref[0], preferred_element_type=F32)
    hidden = (gate / (1.0 + jnp.exp(-gate)) * up).astype(BF16)
    part = jnp.dot(hidden, down_ref[0], preferred_element_type=F32)

    @pl.when(step == 0)
    def _():
        total_ref[...] = part

    @pl.when(step > 0)
    def _():
        total_ref[...] += part

    @pl.when(step == pl.num_programs(0) - 1)
    def _():
        for i in range(count):
            outs[i][...] = total_ref[i * CAP : (i + 1) * CAP, :].astype(BF16)


def run_experts(groups, chunks, width, gain, w_gate, w_up, w_down, blocks):
    count, held = len(blocks), len(blocks[0])
    features, units = w_gate.shape[1:]
    tile = 256 if units % 256 == 0 else 128
    flat = [part for block in blocks for part in block]
    return pl.pallas_call(
        functools.partial(experts_kernel, groups, chunks, width, count, held),
        grid=(units // tile,),
        out_shape=[jax.ShapeDtypeStruct((CAP, features), BF16)] * count,
        in_specs=[
            pl.BlockSpec((1, features), lambda i: (0, 0)),
            pl.BlockSpec((1, features, tile), lambda i: (0, 0, i)),
            pl.BlockSpec((1, features, tile), lambda i: (0, 0, i)),
            pl.BlockSpec((1, tile, features), lambda i: (0, i, 0)),
        ]
        + [pl.BlockSpec(part.shape, lambda i: (0, 0)) for part in flat],
        out_specs=[pl.BlockSpec((CAP, features), lambda i: (0, 0))] * count,
        scratch_shapes=[
            pltpu.VMEM((count * CAP, features), BF16),
            pltpu.VMEM((count * CAP, features), F32),
        ],
        compiler_params=params(32),
        cost_estimate=cost(count * CAP * features, features * units // 100),
        name="experts",
    )(gain, w_gate, w_up, w_down, *flat)


def combine_kernel(groups, experts, widths, ids_ref, gates_ref, *rest):
    chunks = len(widths)
    kept, blocks, out_ref = rest[:chunks], rest[chunks : chunks + experts], rest[-1]
    ids, gates = ids_ref[...], gates_ref[...]
    hits, named = slot_matrix(experts, ids)
    weight = jnp.where(ids[0:1, :] == named, gates[0:1, :], 0.0) + jnp.where(
        ids[1:2, :] == named, gates[1:2, :], 0.0
    )
    coarse = weight.astype(BF16).astype(F32)
    fine = weight - coarse
    spread = []
    for part in (coarse, fine):
        for d in range(experts):
            spread.append(jnp.where(hits[d], part[d : d + 1, :], 0.0).astype(BF16))
    spread = jnp.concatenate(spread, axis=0)
    rows = jnp.concatenate([block[...] for block in blocks], axis=0)
    mixture = lax.dot_general(
        spread,
        jnp.concatenate([rows, rows], axis=0),
        (((0,), (0,)), ((), ())),
        preferred_element_type=F32,
    )
    column = 0
    for g in range(groups):
        for c, w in enumerate(widths):
            part = kept[c][:, g * w : (g + 1) * w].astype(F32)
            out_ref[0, :, column : column + w] = (part + mixture[:, column : column + w]).astype(
                BF16
            )
            column += w


def combine(groups, widths, ids, gates, kept, blocks):
    tokens, features = ids.shape[1], blocks[0].shape[1]
    experts = len(blocks)
    return pl.pallas_call(
        functools.partial(combine_kernel, groups, experts, widths),
        out_shape=jax.ShapeDtypeStruct((1, tokens, features), BF16),
        in_specs=[VMEM] * (2 + len(widths) + experts),
        out_specs=VMEM,
        compiler_params=params(32),
        cost_estimate=cost(4 * experts * CAP * tokens * features, 8 * tokens * features),
        name="combine",
    )(ids, gates, *kept, *blocks)


def after(values, *earlier):
    return lax.optimization_barrier((values, earlier))[0]


def local(
    query_rows, key_rows, value_rows, norm_gain, expert_ids, gate_weights, w_gate, w_up, w_down
):
    features = query_rows.shape[2]
    head_size = features // HEADS
    groups, experts = lax.axis_size("seq"), lax.axis_size("expert")
    per_group = HEADS // groups
    group_width = per_group * head_size
    chunks = CHUNKS if per_group % CHUNKS == 0 else 1
    width = group_width // chunks
    ids, gates = expert_ids[0].T, gate_weights[0].T
    gain = norm_gain.reshape(1, features)
    half = experts // 2
    middle = half + experts // 4

    def exchange(blocks, name):
        with jax.named_scope(name):
            return [blocks[0]] + [swap(blocks[d], "seq", d) for d in range(1, groups)]

    def send(block, distance, name):
        with jax.named_scope(f"{name}{distance}"):
            return swap(block, "expert", distance)

    received = [
        exchange(pack(groups, chunks, c, width, query_rows, key_rows, value_rows), f"qkv{c}_")
        for c in range(chunks)
    ]
    heads = [attend(width, head_size, received[c]) for c in range(chunks)]
    kept, arrived = [], [[] for _ in range(experts)]
    for c in range(chunks):
        last = c == chunks - 1
        out = heads[c] if c == 0 else after(heads[c], kept[-1])
        *rows, own = select(groups, experts, ids, exchange(out, f"heads{c}_"), kept, last)
        kept.append(own)
        for d in range(half, middle):
            row = rows[d - half] if c == 0 else after(rows[d - half], arrived[d][-1])
            arrived[d].append(send(row, d, f"rows{c}_"))
    whole = rows[middle - half :]
    for d in range(middle, experts):
        arrived[d].append(send(whole[d - middle], d, "rows_"))
    whole = whole[experts - middle :]
    arrived[0].append(whole[0])
    for d in range(1, half):
        arrived[d].append(send(whole[d], d, "rows_"))
    returned = [None] * experts
    for members in (range(half, middle), range(middle, experts), range(half)):
        produced = run_experts(
            groups, chunks, width, gain, w_gate, w_up, w_down,
            [arrived[d] for d in members],
        )
        for d, block in zip(members, produced):
            returned[d] = block if d == 0 else send(block, d, "back_")
    return combine(groups, (width,) * chunks, ids, gates, kept, returned)


def solution(mesh):
    rows = P("expert", "seq", None)
    weights = P("expert", None, None)
    return jax.shard_map(
        local,
        mesh=mesh,
        in_specs=(rows, rows, rows, P(), rows, rows, weights, weights, weights),
        out_specs=rows,
        check_vma=False,
    )
```

```python
import functools
import math

import jax
import jax.numpy as jnp
from jax import lax
from jax.experimental import pallas as pl
from jax.experimental.pallas import tpu as pltpu
from jax.sharding import PartitionSpec as P

HEADS = 16
CAP = 32
CHUNKS = 2
PACK_MIB = 56
F32 = jnp.float32
BF16 = jnp.bfloat16
HBM = pl.BlockSpec(memory_space=pltpu.HBM)
VMEM = pl.BlockSpec(memory_space=pltpu.VMEM)


def swap(x, axis, distance):
    size = lax.axis_size(axis)
    return lax.ppermute(x, axis, [(i, i ^ distance) for i in range(size)])


def params(mib):
    return pltpu.CompilerParams(vmem_limit_bytes=mib << 20)


def cost(flops, moved):
    return pl.CostEstimate(flops=flops, bytes_accessed=moved, transcendentals=0)


def pack_kernel(groups, chunks, c, width, q_ref, k_ref, v_ref, *rest):
    outs, (in_sems, *staged) = rest[:groups], rest[groups:]
    me = lax.axis_index("seq")
    inward, outward = [], []
    for distance in [*range(1, groups), 0]:
        column = pl.multiple_of(((me ^ distance) * chunks + c) * width, 128)
        for i, ref in enumerate((q_ref, k_ref, v_ref)):
            n = len(inward)
            target = staged[0].at[n] if staged else outs[distance].at[i]
            inward.append(
                pltpu.make_async_copy(ref.at[0, :, pl.ds(column, width)], target, in_sems.at[n])
            )
            if staged:
                outward.append(
                    pltpu.make_async_copy(target, outs[distance].at[i], staged[1].at[n])
                )
    for copy in inward:
        copy.start()
    for n, copy in enumerate(inward):
        copy.wait()
        if staged:
            outward[n].start()
    for out in outward:
        out.wait()


def pack(groups, chunks, c, width, q, k, v):
    tokens = q.shape[1]
    count = 3 * groups
    staged = [pltpu.VMEM((count, tokens, width), BF16), pltpu.SemaphoreType.DMA((count,))]
    return pl.pallas_call(
        functools.partial(pack_kernel, groups, chunks, c, width),
        out_shape=[jax.ShapeDtypeStruct((3, tokens, width), BF16)] * groups,
        in_specs=[HBM] * 3,
        out_specs=[HBM if c == 0 else VMEM] * groups,
        scratch_shapes=[pltpu.SemaphoreType.DMA((count,))] + (staged if c == 0 else []),
        compiler_params=params(PACK_MIB if c == 0 else 8),
        cost_estimate=cost(0, 4 * count * tokens * width),
        name="pack_heads",
    )(q, k, v)


def attend_kernel(groups, width, head_size, *rest):
    blocks, outs = rest[:groups], rest[groups:]
    scale = head_size**-0.5 * math.log2(math.e)
    step = min(groups, 4)
    for head in range(width // head_size):
        lanes = slice(head * head_size, (head + 1) * head_size)
        keys = jnp.concatenate([block[1, :, lanes] for block in blocks], axis=0)
        values = jnp.concatenate([block[2, :, lanes] for block in blocks], axis=0)
        for first in range(0, groups, step):
            members = range(first, min(first + step, groups))
            scores = [
                lax.dot_general(
                    blocks[b][0, :, lanes], keys, (((1,), (1,)), ((), ())),
                    preferred_element_type=F32,
                )
                for b in members
            ]
            peaks = [jnp.max(part, axis=-1, keepdims=True) for part in scores]
            exponentials = [jnp.exp2((s - p) * scale) for s, p in zip(scores, peaks)]
            totals = [jnp.sum(part, axis=-1, keepdims=True) for part in exponentials]
            weighted = [
                jnp.dot(part.astype(BF16), values, preferred_element_type=F32)
                for part in exponentials
            ]
            for b, part, total in zip(members, weighted, totals):
                outs[b][:, lanes] = (part * (1.0 / total)).astype(BF16)


def attend(width, head_size, blocks):
    groups, tokens = len(blocks), blocks[0].shape[1]
    total = groups * tokens
    return pl.pallas_call(
        functools.partial(attend_kernel, groups, width, head_size),
        out_shape=[jax.ShapeDtypeStruct((tokens, width), BF16)] * groups,
        in_specs=[VMEM] * groups,
        out_specs=[VMEM] * groups,
        compiler_params=params(32),
        cost_estimate=cost(160 * total * total * width, 80 * total * width),
        name="attend",
    )(*blocks)


def slot_matrix(experts, ids):
    tokens = ids.shape[1]
    me = lax.axis_index("expert")
    named = lax.broadcasted_iota(jnp.int32, (experts, tokens), 0) ^ me
    matches = jnp.where((ids[0:1, :] == named) | (ids[1:2, :] == named), 1.0, 0.0)
    earlier = jnp.where(
        lax.broadcasted_iota(jnp.int32, (tokens, tokens), 0)
        < lax.broadcasted_iota(jnp.int32, (tokens, tokens), 1),
        1.0,
        0.0,
    )
    rank = jnp.dot(matches.astype(BF16), earlier.astype(BF16), preferred_element_type=F32)
    rank = jnp.where(matches > 0.0, rank, -1.0).astype(jnp.int32)
    slots = lax.broadcasted_iota(jnp.int32, (CAP, tokens), 0)
    return [slots == rank[d : d + 1, :] for d in range(experts)], named


def select_kernel(groups, experts, width, earlier, last, ids_ref, *rest):
    blocks, before = rest[:groups], rest[groups : groups + earlier]
    half, middle = experts // 2, experts // 2 + experts // 4
    count = experts if last else middle - half
    outs = rest[groups + earlier : groups + earlier + count]
    kept, sems = rest[groups + earlier + count :]
    me = lax.axis_index("seq")
    copies = []
    for d in range(groups):
        column = pl.multiple_of((me ^ d) * width, 128)
        copies.append(
            pltpu.make_async_copy(blocks[d], kept.at[:, pl.ds(column, width)], sems.at[d])
        )
    for copy in copies:
        copy.start()
    hits, _ = slot_matrix(experts, ids_ref[...])
    chosen = [jnp.where(h, 1.0, 0.0).astype(BF16) for h in hits]
    for copy in copies:
        copy.wait()

    def pick(distances, rows, first):
        picked = jnp.dot(
            jnp.concatenate([chosen[d] for d in distances], axis=0),
            rows,
            preferred_element_type=F32,
        ).astype(BF16)
        for i in range(len(distances)):
            outs[first + i][...] = picked[i * CAP : (i + 1) * CAP]

    pick(range(half, middle), kept[...], 0)
    if last:
        parts = [ref[...] for ref in before] + [kept[...]]
        full = jnp.concatenate(parts, axis=1) if earlier else parts[0]
        pick([*range(middle, experts), *range(half)], full, middle - half)


def select(groups, experts, ids, blocks, before, last):
    tokens, width = blocks[0].shape
    part = groups * width
    whole = part * (len(before) + 1)
    quarter = experts // 4
    shapes = [(CAP, part)] * quarter
    if last:
        shapes += [(CAP, whole)] * (experts - quarter)
    shapes.append((tokens, part))
    return pl.pallas_call(
        functools.partial(select_kernel, groups, experts, width, len(before), last),
        out_shape=[jax.ShapeDtypeStruct(shape, BF16) for shape in shapes],
        in_specs=[VMEM] + [HBM] * groups + [VMEM] * len(before),
        out_specs=[VMEM] * len(shapes),
        scratch_shapes=[pltpu.SemaphoreType.DMA((groups,))],
        compiler_params=params(16),
        cost_estimate=cost(2 * experts * CAP * tokens * part, 8 * tokens * part),
        name="select_rows",
    )(ids, *blocks, *before)


def experts_kernel(groups, chunks, width, held, gain_ref, gate_ref, up_ref, down_ref, *rest):
    inputs, count = sum(held), len(held)
    blocks, outs = rest[:inputs], rest[inputs : inputs + count]
    rows_ref, hidden_ref = rest[inputs + count :]
    used = 0
    for i in range(count):
        mine = [blocks[k][...] for k in range(used, used + held[i])]
        used += held[i]
        row = jnp.concatenate(mine, axis=1) if len(mine) > 1 else mine[0]
        parts = []
        for g in range(groups):
            for c in range(chunks):
                first = (c * groups + g) * width
                parts.append(row[:, first : first + width].astype(F32))
        row = jnp.concatenate(parts, axis=1)
        scale = lax.rsqrt(jnp.mean(row * row, axis=-1, keepdims=True) + 1e-06)
        rows_ref[i * CAP : (i + 1) * CAP, :] = (row * scale * gain_ref[...]).astype(BF16)
    units, features = down_ref.shape[1:]
    tile = 256 if units % 256 == 0 else 128
    for first in range(0, units, tile):
        lanes = slice(first, first + tile)
        gate = jnp.dot(rows_ref[...], gate_ref[0, :, lanes], preferred_element_type=F32)
        up = jnp.dot(rows_ref[...], up_ref[0, :, lanes], preferred_element_type=F32)
        hidden_ref[:, lanes] = (gate / (1.0 + jnp.exp(-gate)) * up).astype(BF16)
    for first in range(0, features, 512):
        lanes = slice(first, first + 512)
        made = jnp.dot(hidden_ref[...], down_ref[0, :, lanes], preferred_element_type=F32)
        for i in range(count):
            outs[i][:, lanes] = made[i * CAP : (i + 1) * CAP].astype(BF16)


def run_experts(groups, chunks, width, gain, w_gate, w_up, w_down, blocks):
    held = tuple(len(block) for block in blocks)
    count = len(held)
    features, units = w_gate.shape[1:]
    flat = [part for block in blocks for part in block]
    return pl.pallas_call(
        functools.partial(experts_kernel, groups, chunks, width, held),
        out_shape=[jax.ShapeDtypeStruct((CAP, features), BF16)] * count,
        in_specs=[VMEM] * (4 + len(flat)),
        out_specs=[VMEM] * count,
        scratch_shapes=[
            pltpu.VMEM((count * CAP, features), BF16),
            pltpu.VMEM((count * CAP, units), BF16),
        ],
        compiler_params=params(24),
        cost_estimate=cost(count * CAP * features, features * units // 100),
        name="experts",
    )(gain, w_gate, w_up, w_down, *flat)


def spread_kernel(experts, ids_ref, gates_ref, coarse_ref, fine_ref):
    ids, gates = ids_ref[...], gates_ref[...]
    hits, named = slot_matrix(experts, ids)
    weight = jnp.where(ids[0:1, :] == named, gates[0:1, :], 0.0) + jnp.where(
        ids[1:2, :] == named, gates[1:2, :], 0.0
    )
    coarse = weight.astype(BF16).astype(F32)
    for ref, part in ((coarse_ref, coarse), (fine_ref, weight - coarse)):
        slots = [jnp.where(hits[d], part[d : d + 1, :], 0.0) for d in range(experts)]
        ref[...] = jnp.concatenate(slots, axis=0).T.astype(BF16)


def spread(experts, ids, gates):
    tokens = ids.shape[1]
    return pl.pallas_call(
        functools.partial(spread_kernel, experts),
        out_shape=[jax.ShapeDtypeStruct((tokens, experts * CAP), BF16)] * 2,
        in_specs=[VMEM] * 2,
        out_specs=[VMEM] * 2,
        compiler_params=params(16),
        cost_estimate=cost(0, 4 * tokens * experts * CAP),
        name="spread_gates",
    )(ids, gates)


def combine_kernel(groups, experts, chunks, coarse_ref, fine_ref, *rest):
    kept, blocks = rest[:chunks], rest[chunks : chunks + experts]
    out_ref, made_ref, sems = rest[chunks + experts :]
    width = kept[0].shape[1] // groups
    copies = []
    for g in range(groups):
        span = slice(g * chunks * width, (g + 1) * chunks * width)
        rows = jnp.concatenate([block[:, span] for block in blocks], axis=0)
        total = jnp.concatenate(
            [ref[:, g * width : (g + 1) * width] for ref in kept], axis=1
        ).astype(F32)
        total += jnp.dot(coarse_ref[...], rows, preferred_element_type=F32)
        total += jnp.dot(fine_ref[...], rows, preferred_element_type=F32)
        made_ref[:, span] = total.astype(BF16)
        copies.append(
            pltpu.make_async_copy(made_ref.at[:, span], out_ref.at[0, :, span], sems.at[g])
        )
        copies[-1].start()
    for copy in copies:
        copy.wait()


def combine(groups, weights, kept, blocks):
    tokens, features = weights[0].shape[0], blocks[0].shape[1]
    experts = len(blocks)
    return pl.pallas_call(
        functools.partial(combine_kernel, groups, experts, len(kept)),
        out_shape=jax.ShapeDtypeStruct((1, tokens, features), BF16),
        in_specs=[VMEM] * (2 + len(kept) + experts),
        out_specs=HBM,
        scratch_shapes=[
            pltpu.VMEM((tokens, features), BF16),
            pltpu.SemaphoreType.DMA((groups,)),
        ],
        compiler_params=params(24),
        cost_estimate=cost(4 * experts * CAP * tokens * features, 8 * tokens * features),
        name="combine",
    )(*weights, *kept, *blocks)


def after(values, *earlier):
    return lax.optimization_barrier((values, earlier))[0]


def local(
    query_rows, key_rows, value_rows, norm_gain, expert_ids, gate_weights, w_gate, w_up, w_down
):
    features = query_rows.shape[2]
    head_size = features // HEADS
    groups, experts = lax.axis_size("seq"), lax.axis_size("expert")
    per_group = HEADS // groups
    group_width = per_group * head_size
    chunks = CHUNKS if per_group % CHUNKS == 0 else 1
    width = group_width // chunks
    ids, gates = expert_ids[0].T, gate_weights[0].T
    gain = norm_gain.reshape(1, features)
    half = experts // 2
    middle = half + experts // 4

    def exchange(blocks, name):
        with jax.named_scope(name):
            return [blocks[0]] + [swap(blocks[d], "seq", d) for d in range(1, groups)]

    def send(block, distance, name):
        with jax.named_scope(f"{name}{distance}"):
            return swap(block, "expert", distance)

    received = [
        exchange(pack(groups, chunks, c, width, query_rows, key_rows, value_rows), f"qkv{c}_")
        for c in range(chunks)
    ]
    weights = spread(experts, ids, gates)
    received[-1][0] = after(received[-1][0], weights)
    heads = [attend(width, head_size, received[c]) for c in range(chunks)]
    kept, arrived = [], [[] for _ in range(experts)]
    for c in range(chunks):
        last = c == chunks - 1
        out = heads[c] if c == 0 else after(heads[c], kept[-1])
        *rows, own = select(groups, experts, ids, exchange(out, f"heads{c}_"), kept, last)
        kept.append(own)
        for d in range(half, middle):
            row = rows[d - half] if c == 0 else after(rows[d - half], arrived[d][-1])
            arrived[d].append(send(row, d, f"rows{c}_"))
    whole = rows[middle - half :]
    for d in range(middle, experts):
        arrived[d].append(send(whole[d - middle], d, "rows_"))
    whole = whole[experts - middle :]
    arrived[0].append(whole[0])
    for d in range(1, half):
        arrived[d].append(send(whole[d], d, "rows_"))
    returned = [None] * experts
    for members in (range(half, middle), range(middle, experts), range(half)):
        produced = run_experts(
            groups, chunks, width, gain, w_gate, w_up, w_down,
            [arrived[d] for d in members],
        )
        for d, block in zip(members, produced):
            returned[d] = block if d == 0 else send(block, d, "back_")
    return combine(groups, weights, kept, returned)


def solution(mesh):
    rows = P("expert", "seq", None)
    weights = P("expert", None, None)
    return jax.shard_map(
        local,
        mesh=mesh,
        in_specs=(rows, rows, rows, P(), rows, rows, weights, weights, weights),
        out_specs=rows,
        check_vma=False,
    )
```

```python
import functools
import math

import jax
import jax.numpy as jnp
from jax import lax
from jax.experimental import pallas as pl
from jax.experimental.pallas import tpu as pltpu
from jax.sharding import PartitionSpec as P

HEADS = 16
CAP = 32
CHUNKS = 2
PACK_MIB = 53
F32 = jnp.float32
BF16 = jnp.bfloat16
HBM = pl.BlockSpec(memory_space=pltpu.HBM)
VMEM = pl.BlockSpec(memory_space=pltpu.VMEM)


def swap(x, axis, distance):
    size = lax.axis_size(axis)
    return lax.ppermute(x, axis, [(i, i ^ distance) for i in range(size)])


def params(mib):
    return pltpu.CompilerParams(vmem_limit_bytes=mib << 20)


def cost(flops, moved):
    return pl.CostEstimate(flops=flops, bytes_accessed=moved, transcendentals=0)


def pack_kernel(places, chunks, width, q_ref, k_ref, v_ref, *rest):
    outs, sems = rest[:-1], rest[-1]
    me = lax.axis_index("seq")
    copies = []
    for out, (distance, c) in zip(outs, places):
        column = pl.multiple_of(((me ^ distance) * chunks + c) * width, 128)
        for i, ref in enumerate((q_ref, k_ref, v_ref)):
            copies.append(
                pltpu.make_async_copy(
                    ref.at[0, :, pl.ds(column, width)], out.at[i], sems.at[len(copies)]
                )
            )
    for copy in copies:
        copy.start()
    for copy in copies:
        copy.wait()


def pack(places, chunks, width, mib, q, k, v):
    tokens = q.shape[1]
    count = 3 * len(places)
    return pl.pallas_call(
        functools.partial(pack_kernel, places, chunks, width),
        out_shape=[jax.ShapeDtypeStruct((3, tokens, width), BF16)] * len(places),
        in_specs=[HBM] * 3,
        out_specs=[VMEM] * len(places),
        scratch_shapes=[pltpu.SemaphoreType.DMA((count,))],
        compiler_params=params(mib),
        cost_estimate=cost(0, 4 * count * tokens * width),
        name="pack_heads",
    )(q, k, v)


def attend_kernel(groups, width, head_size, *rest):
    blocks, outs = rest[:groups], rest[groups:]
    scale = head_size**-0.5 * math.log2(math.e)
    step = min(groups, 4)
    for head in range(width // head_size):
        lanes = slice(head * head_size, (head + 1) * head_size)
        keys = jnp.concatenate([block[1, :, lanes] for block in blocks], axis=0)
        values = jnp.concatenate([block[2, :, lanes] for block in blocks], axis=0)
        for first in range(0, groups, step):
            members = range(first, min(first + step, groups))
            scores = [
                lax.dot_general(
                    blocks[b][0, :, lanes], keys, (((1,), (1,)), ((), ())),
                    preferred_element_type=F32,
                )
                for b in members
            ]
            peaks = [jnp.max(part, axis=-1, keepdims=True) for part in scores]
            exponentials = [jnp.exp2((s - p) * scale) for s, p in zip(scores, peaks)]
            totals = [jnp.sum(part, axis=-1, keepdims=True) for part in exponentials]
            weighted = [
                jnp.dot(part.astype(BF16), values, preferred_element_type=F32)
                for part in exponentials
            ]
            for b, part, total in zip(members, weighted, totals):
                outs[b][:, lanes] = (part * (1.0 / total)).astype(BF16)


def attend(width, head_size, blocks):
    groups, tokens = len(blocks), blocks[0].shape[1]
    total = groups * tokens
    return pl.pallas_call(
        functools.partial(attend_kernel, groups, width, head_size),
        out_shape=[jax.ShapeDtypeStruct((tokens, width), BF16)] * groups,
        in_specs=[VMEM] * groups,
        out_specs=[VMEM] * groups,
        compiler_params=params(32),
        cost_estimate=cost(160 * total * total * width, 80 * total * width),
        name="attend",
    )(*blocks)


def slot_matrix(experts, ids):
    tokens = ids.shape[1]
    me = lax.axis_index("expert")
    named = lax.broadcasted_iota(jnp.int32, (experts, tokens), 0) ^ me
    matches = jnp.where((ids[0:1, :] == named) | (ids[1:2, :] == named), 1.0, 0.0)
    earlier = jnp.where(
        lax.broadcasted_iota(jnp.int32, (tokens, tokens), 0)
        < lax.broadcasted_iota(jnp.int32, (tokens, tokens), 1),
        1.0,
        0.0,
    )
    rank = jnp.dot(matches.astype(BF16), earlier.astype(BF16), preferred_element_type=F32)
    rank = jnp.where(matches > 0.0, rank, -1.0).astype(jnp.int32)
    slots = lax.broadcasted_iota(jnp.int32, (CAP, tokens), 0)
    return [slots == rank[d : d + 1, :] for d in range(experts)], named


def select_kernel(groups, experts, width, earlier, last, ids_ref, *rest):
    blocks, before = rest[:groups], rest[groups : groups + earlier]
    half, middle = experts // 2, experts // 2 + experts // 4
    count = experts if last else middle - half
    outs = rest[groups + earlier : groups + earlier + count]
    kept, sems = rest[groups + earlier + count :]
    me = lax.axis_index("seq")
    copies = []
    for d in range(groups):
        column = pl.multiple_of((me ^ d) * width, 128)
        copies.append(
            pltpu.make_async_copy(blocks[d], kept.at[:, pl.ds(column, width)], sems.at[d])
        )
    for copy in copies:
        copy.start()
    hits, _ = slot_matrix(experts, ids_ref[...])
    chosen = [jnp.where(h, 1.0, 0.0).astype(BF16) for h in hits]
    for copy in copies:
        copy.wait()

    def pick(distances, rows, first):
        picked = jnp.dot(
            jnp.concatenate([chosen[d] for d in distances], axis=0),
            rows,
            preferred_element_type=F32,
        ).astype(BF16)
        for i in range(len(distances)):
            outs[first + i][...] = picked[i * CAP : (i + 1) * CAP]

    pick(range(half, middle), kept[...], 0)
    if last:
        parts = [ref[...] for ref in before] + [kept[...]]
        full = jnp.concatenate(parts, axis=1) if earlier else parts[0]
        pick([*range(middle, experts), *range(half)], full, middle - half)


def select(groups, experts, ids, blocks, before, last):
    tokens, width = blocks[0].shape
    part = groups * width
    whole = part * (len(before) + 1)
    quarter = experts // 4
    shapes = [(CAP, part)] * quarter
    if last:
        shapes += [(CAP, whole)] * (experts - quarter)
    shapes.append((tokens, part))
    return pl.pallas_call(
        functools.partial(select_kernel, groups, experts, width, len(before), last),
        out_shape=[jax.ShapeDtypeStruct(shape, BF16) for shape in shapes],
        in_specs=[VMEM] + [HBM] * groups + [VMEM] * len(before),
        out_specs=[VMEM] * len(shapes),
        scratch_shapes=[pltpu.SemaphoreType.DMA((groups,))],
        compiler_params=params(16),
        cost_estimate=cost(2 * experts * CAP * tokens * part, 8 * tokens * part),
        name="select_rows",
    )(ids, *blocks, *before)


def experts_kernel(groups, chunks, width, held, gain_ref, gate_ref, up_ref, down_ref, *rest):
    inputs, count = sum(held), len(held)
    blocks, outs = rest[:inputs], rest[inputs : inputs + count]
    rows_ref, hidden_ref = rest[inputs + count :]
    used = 0
    for i in range(count):
        mine = [blocks[k][...] for k in range(used, used + held[i])]
        used += held[i]
        row = jnp.concatenate(mine, axis=1) if len(mine) > 1 else mine[0]
        parts = []
        for g in range(groups):
            for c in range(chunks):
                first = (c * groups + g) * width
                parts.append(row[:, first : first + width].astype(F32))
        row = jnp.concatenate(parts, axis=1)
        scale = lax.rsqrt(jnp.mean(row * row, axis=-1, keepdims=True) + 1e-06)
        rows_ref[i * CAP : (i + 1) * CAP, :] = (row * scale * gain_ref[...]).astype(BF16)
    units, features = down_ref.shape[1:]
    tile = 256 if units % 256 == 0 else 128
    for first in range(0, units, tile):
        lanes = slice(first, first + tile)
        gate = jnp.dot(rows_ref[...], gate_ref[0, :, lanes], preferred_element_type=F32)
        up = jnp.dot(rows_ref[...], up_ref[0, :, lanes], preferred_element_type=F32)
        hidden_ref[:, lanes] = (gate / (1.0 + jnp.exp(-gate)) * up).astype(BF16)
    for first in range(0, features, 512):
        lanes = slice(first, first + 512)
        made = jnp.dot(hidden_ref[...], down_ref[0, :, lanes], preferred_element_type=F32)
        for i in range(count):
            outs[i][:, lanes] = made[i * CAP : (i + 1) * CAP].astype(BF16)


def run_experts(groups, chunks, width, gain, w_gate, w_up, w_down, blocks):
    held = tuple(len(block) for block in blocks)
    count = len(held)
    features, units = w_gate.shape[1:]
    flat = [part for block in blocks for part in block]
    return pl.pallas_call(
        functools.partial(experts_kernel, groups, chunks, width, held),
        out_shape=[jax.ShapeDtypeStruct((CAP, features), BF16)] * count,
        in_specs=[VMEM] * (4 + len(flat)),
        out_specs=[VMEM] * count,
        scratch_shapes=[
            pltpu.VMEM((count * CAP, features), BF16),
            pltpu.VMEM((count * CAP, units), BF16),
        ],
        compiler_params=params(24),
        cost_estimate=cost(count * CAP * features, features * units // 100),
        name="experts",
    )(gain, w_gate, w_up, w_down, *flat)


def spread_kernel(experts, ids_ref, gates_ref, coarse_ref, fine_ref):
    ids, gates = ids_ref[...], gates_ref[...]
    hits, named = slot_matrix(experts, ids)
    weight = jnp.where(ids[0:1, :] == named, gates[0:1, :], 0.0) + jnp.where(
        ids[1:2, :] == named, gates[1:2, :], 0.0
    )
    coarse = weight.astype(BF16).astype(F32)
    for ref, part in ((coarse_ref, coarse), (fine_ref, weight - coarse)):
        slots = [jnp.where(hits[d], part[d : d + 1, :], 0.0) for d in range(experts)]
        ref[...] = jnp.concatenate(slots, axis=0).T.astype(BF16)


def spread(experts, ids, gates):
    tokens = ids.shape[1]
    return pl.pallas_call(
        functools.partial(spread_kernel, experts),
        out_shape=[jax.ShapeDtypeStruct((tokens, experts * CAP), BF16)] * 2,
        in_specs=[VMEM] * 2,
        out_specs=[VMEM] * 2,
        compiler_params=params(16),
        cost_estimate=cost(0, 4 * tokens * experts * CAP),
        name="spread_gates",
    )(ids, gates)


def combine_kernel(groups, experts, chunks, coarse_ref, fine_ref, *rest):
    kept, blocks = rest[:chunks], rest[chunks : chunks + experts]
    out_ref, made_ref, sems = rest[chunks + experts :]
    width = kept[0].shape[1] // groups
    copies = []
    for g in range(groups):
        span = slice(g * chunks * width, (g + 1) * chunks * width)
        rows = jnp.concatenate([block[:, span] for block in blocks], axis=0)
        total = jnp.concatenate(
            [ref[:, g * width : (g + 1) * width] for ref in kept], axis=1
        ).astype(F32)
        total += jnp.dot(coarse_ref[...], rows, preferred_element_type=F32)
        total += jnp.dot(fine_ref[...], rows, preferred_element_type=F32)
        made_ref[:, span] = total.astype(BF16)
        copies.append(
            pltpu.make_async_copy(made_ref.at[:, span], out_ref.at[0, :, span], sems.at[g])
        )
        copies[-1].start()
    for copy in copies:
        copy.wait()


def combine(groups, weights, kept, blocks):
    tokens, features = weights[0].shape[0], blocks[0].shape[1]
    experts = len(blocks)
    return pl.pallas_call(
        functools.partial(combine_kernel, groups, experts, len(kept)),
        out_shape=jax.ShapeDtypeStruct((1, tokens, features), BF16),
        in_specs=[VMEM] * (2 + len(kept) + experts),
        out_specs=HBM,
        scratch_shapes=[
            pltpu.VMEM((tokens, features), BF16),
            pltpu.SemaphoreType.DMA((groups,)),
        ],
        compiler_params=params(24),
        cost_estimate=cost(4 * experts * CAP * tokens * features, 8 * tokens * features),
        name="combine",
    )(*weights, *kept, *blocks)


def after(values, *earlier):
    return lax.optimization_barrier((values, earlier))[0]


def local(
    query_rows, key_rows, value_rows, norm_gain, expert_ids, gate_weights, w_gate, w_up, w_down
):
    features = query_rows.shape[2]
    head_size = features // HEADS
    groups, experts = lax.axis_size("seq"), lax.axis_size("expert")
    per_group = HEADS // groups
    group_width = per_group * head_size
    chunks = CHUNKS if per_group % CHUNKS == 0 else 1
    width = group_width // chunks
    ids, gates = expert_ids[0].T, gate_weights[0].T
    gain = norm_gain.reshape(1, features)
    half = experts // 2
    middle = half + experts // 4

    def exchange(blocks, name):
        with jax.named_scope(name):
            return [blocks[0]] + [swap(blocks[d], "seq", d) for d in range(1, groups)]

    def send(block, distance, name):
        with jax.named_scope(f"{name}{distance}"):
            return swap(block, "expert", distance)

    first = [(d, 0) for d in range(1, groups)]
    others = [(0, 0)] + [(d, c) for c in range(1, chunks) for d in range(groups)]
    packed = pack(first, chunks, width, PACK_MIB, query_rows, key_rows, value_rows)
    own, *rest = pack(others, chunks, width, 8, query_rows, key_rows, value_rows)
    packed = [own, *packed, *rest]
    received = [
        exchange(packed[c * groups : (c + 1) * groups], f"qkv{c}_") for c in range(chunks)
    ]
    weights = spread(experts, ids, gates)
    received[-1][0] = after(received[-1][0], weights)
    heads = [attend(width, head_size, received[c]) for c in range(chunks)]
    kept, arrived = [], [[] for _ in range(experts)]
    for c in range(chunks):
        last = c == chunks - 1
        out = heads[c]
        *rows, own = select(groups, experts, ids, exchange(out, f"heads{c}_"), kept, last)
        kept.append(own)
        for d in range(half, middle):
            row = rows[d - half] if c == 0 else after(rows[d - half], arrived[d][-1])
            arrived[d].append(send(row, d, f"rows{c}_"))
    whole = rows[middle - half :]
    for d in range(middle, experts):
        arrived[d].append(send(whole[d - middle], d, "rows_"))
    whole = whole[experts - middle :]
    arrived[0].append(whole[0])
    for d in range(1, half):
        arrived[d].append(send(whole[d], d, "rows_"))
    returned = [None] * experts
    for members in (range(half, middle), range(middle, experts), range(half)):
        produced = run_experts(
            groups, chunks, width, gain, w_gate, w_up, w_down,
            [arrived[d] for d in members],
        )
        for d, block in zip(members, produced):
            returned[d] = block if d == 0 else send(block, d, "back_")
    return combine(groups, weights, kept, returned)


def solution(mesh):
    rows = P("expert", "seq", None)
    weights = P("expert", None, None)
    return jax.shard_map(
        local,
        mesh=mesh,
        in_specs=(rows, rows, rows, P(), rows, rows, weights, weights, weights),
        out_specs=rows,
        check_vma=False,
    )
```

```python
import functools
import math

import jax
import jax.numpy as jnp
from jax import lax
from jax.experimental import pallas as pl
from jax.experimental.pallas import tpu as pltpu
from jax.sharding import PartitionSpec as P

HEADS = 16
CAP = 32
CHUNKS = 2
PACK_MIB = 53
F32 = jnp.float32
BF16 = jnp.bfloat16
HBM = pl.BlockSpec(memory_space=pltpu.HBM)
VMEM = pl.BlockSpec(memory_space=pltpu.VMEM)


def swap(x, axis, distance):
    size = lax.axis_size(axis)
    return lax.ppermute(x, axis, [(i, i ^ distance) for i in range(size)])


def params(mib):
    return pltpu.CompilerParams(vmem_limit_bytes=mib << 20)


def cost(flops, moved):
    return pl.CostEstimate(flops=flops, bytes_accessed=moved, transcendentals=0)


def pack_kernel(places, chunks, width, q_ref, k_ref, v_ref, *rest):
    outs, sems = rest[:-1], rest[-1]
    me = lax.axis_index("seq")
    copies = []
    for out, (distance, c) in zip(outs, places):
        column = pl.multiple_of(((me ^ distance) * chunks + c) * width, 128)
        for i, ref in enumerate((q_ref, k_ref, v_ref)):
            copies.append(
                pltpu.make_async_copy(
                    ref.at[0, :, pl.ds(column, width)], out.at[i], sems.at[len(copies)]
                )
            )
    for copy in copies:
        copy.start()
    for copy in copies:
        copy.wait()


def pack(places, chunks, width, mib, q, k, v):
    tokens = q.shape[1]
    count = 3 * len(places)
    return pl.pallas_call(
        functools.partial(pack_kernel, places, chunks, width),
        out_shape=[jax.ShapeDtypeStruct((3, tokens, width), BF16)] * len(places),
        in_specs=[HBM] * 3,
        out_specs=[VMEM] * len(places),
        scratch_shapes=[pltpu.SemaphoreType.DMA((count,))],
        compiler_params=params(mib),
        cost_estimate=cost(0, 4 * count * tokens * width),
        name="pack_heads",
    )(q, k, v)


def attend_kernel(groups, width, head_size, *rest):
    blocks, outs = rest[:groups], rest[groups:]
    scale = head_size**-0.5 * math.log2(math.e)
    step = min(groups, 4)
    for head in range(width // head_size):
        lanes = slice(head * head_size, (head + 1) * head_size)
        keys = jnp.concatenate([block[1, :, lanes] for block in blocks], axis=0)
        values = jnp.concatenate([block[2, :, lanes] for block in blocks], axis=0)
        for first in range(0, groups, step):
            members = range(first, min(first + step, groups))
            scores = [
                lax.dot_general(
                    blocks[b][0, :, lanes], keys, (((1,), (1,)), ((), ())),
                    preferred_element_type=F32,
                )
                for b in members
            ]
            peaks = [jnp.max(part, axis=-1, keepdims=True) for part in scores]
            exponentials = [jnp.exp2((s - p) * scale) for s, p in zip(scores, peaks)]
            totals = [jnp.sum(part, axis=-1, keepdims=True) for part in exponentials]
            weighted = [
                jnp.dot(part.astype(BF16), values, preferred_element_type=F32)
                for part in exponentials
            ]
            for b, part, total in zip(members, weighted, totals):
                outs[b][:, lanes] = (part * (1.0 / total)).astype(BF16)


def attend(width, head_size, blocks):
    groups, tokens = len(blocks), blocks[0].shape[1]
    total = groups * tokens
    return pl.pallas_call(
        functools.partial(attend_kernel, groups, width, head_size),
        out_shape=[jax.ShapeDtypeStruct((tokens, width), BF16)] * groups,
        in_specs=[VMEM] * groups,
        out_specs=[VMEM] * groups,
        compiler_params=params(32),
        cost_estimate=cost(160 * total * total * width, 80 * total * width),
        name="attend",
    )(*blocks)


def slot_matrix(experts, ids):
    tokens = ids.shape[1]
    me = lax.axis_index("expert")
    named = lax.broadcasted_iota(jnp.int32, (experts, tokens), 0) ^ me
    matches = jnp.where((ids[0:1, :] == named) | (ids[1:2, :] == named), 1.0, 0.0)
    earlier = jnp.where(
        lax.broadcasted_iota(jnp.int32, (tokens, tokens), 0)
        < lax.broadcasted_iota(jnp.int32, (tokens, tokens), 1),
        1.0,
        0.0,
    )
    rank = jnp.dot(matches.astype(BF16), earlier.astype(BF16), preferred_element_type=F32)
    rank = jnp.where(matches > 0.0, rank, -1.0).astype(jnp.int32)
    slots = lax.broadcasted_iota(jnp.int32, (CAP, tokens), 0)
    return [slots == rank[d : d + 1, :] for d in range(experts)], named


def select_kernel(groups, experts, width, earlier, last, chosen_ref, *rest):
    blocks, before = rest[:groups], rest[groups : groups + earlier]
    half, middle = experts // 2, experts // 2 + experts // 4
    count = experts if last else middle - half
    outs = rest[groups + earlier : groups + earlier + count]
    kept = rest[groups + earlier + count]
    me = lax.axis_index("seq")
    for d in range(groups):
        column = pl.multiple_of((me ^ d) * width, 128)
        kept[:, pl.ds(column, width)] = blocks[d][...]

    def pick(low, high, rows, targets):
        picked = jnp.dot(
            chosen_ref[low * CAP : high * CAP], rows, preferred_element_type=F32
        ).astype(BF16)
        for i, target in enumerate(targets):
            target[...] = picked[i * CAP : (i + 1) * CAP]

    pick(half, middle, kept[...], outs[: middle - half])
    if last:
        parts = [ref[...] for ref in before] + [kept[...]]
        full = jnp.concatenate(parts, axis=1) if earlier else parts[0]
        pick(middle, experts, full, outs[middle - half : experts - half])
        pick(0, half, full, outs[experts - half :])


def select(groups, experts, chosen, blocks, before, last):
    tokens, width = blocks[0].shape
    part = groups * width
    whole = part * (len(before) + 1)
    quarter = experts // 4
    shapes = [(CAP, part)] * quarter
    if last:
        shapes += [(CAP, whole)] * (experts - quarter)
    shapes.append((tokens, part))
    return pl.pallas_call(
        functools.partial(select_kernel, groups, experts, width, len(before), last),
        out_shape=[jax.ShapeDtypeStruct(shape, BF16) for shape in shapes],
        in_specs=[VMEM] * (1 + groups + len(before)),
        out_specs=[VMEM] * len(shapes),
        compiler_params=params(16),
        cost_estimate=cost(2 * experts * CAP * tokens * part, 8 * tokens * part),
        name="select_rows",
    )(chosen, *blocks, *before)


def experts_kernel(groups, chunks, width, held, gain_ref, gate_ref, up_ref, down_ref, *rest):
    inputs, count = sum(held), len(held)
    blocks, outs = rest[:inputs], rest[inputs : inputs + count]
    rows_ref, hidden_ref = rest[inputs + count :]
    used = 0
    for i in range(count):
        mine = [blocks[k][...] for k in range(used, used + held[i])]
        used += held[i]
        row = jnp.concatenate(mine, axis=1) if len(mine) > 1 else mine[0]
        parts = []
        for g in range(groups):
            for c in range(chunks):
                first = (c * groups + g) * width
                parts.append(row[:, first : first + width].astype(F32))
        row = jnp.concatenate(parts, axis=1)
        scale = lax.rsqrt(jnp.mean(row * row, axis=-1, keepdims=True) + 1e-06)
        rows_ref[i * CAP : (i + 1) * CAP, :] = (row * scale * gain_ref[...]).astype(BF16)
    units, features = down_ref.shape[1:]
    tile = 256 if units % 256 == 0 else 128
    for first in range(0, units, tile):
        lanes = slice(first, first + tile)
        gate = jnp.dot(rows_ref[...], gate_ref[0, :, lanes], preferred_element_type=F32)
        up = jnp.dot(rows_ref[...], up_ref[0, :, lanes], preferred_element_type=F32)
        hidden_ref[:, lanes] = (gate / (1.0 + jnp.exp(-gate)) * up).astype(BF16)
    for first in range(0, features, 512):
        lanes = slice(first, first + 512)
        made = jnp.dot(hidden_ref[...], down_ref[0, :, lanes], preferred_element_type=F32)
        for i in range(count):
            outs[i][:, lanes] = made[i * CAP : (i + 1) * CAP].astype(BF16)


def run_experts(groups, chunks, width, gain, w_gate, w_up, w_down, blocks):
    held = tuple(len(block) for block in blocks)
    count = len(held)
    features, units = w_gate.shape[1:]
    flat = [part for block in blocks for part in block]
    return pl.pallas_call(
        functools.partial(experts_kernel, groups, chunks, width, held),
        out_shape=[jax.ShapeDtypeStruct((CAP, features), BF16)] * count,
        in_specs=[VMEM] * (4 + len(flat)),
        out_specs=[VMEM] * count,
        scratch_shapes=[
            pltpu.VMEM((count * CAP, features), BF16),
            pltpu.VMEM((count * CAP, units), BF16),
        ],
        compiler_params=params(24),
        cost_estimate=cost(count * CAP * features, features * units // 100),
        name="experts",
    )(gain, w_gate, w_up, w_down, *flat)


def spread_kernel(experts, ids_ref, gates_ref, coarse_ref, fine_ref, chosen_ref):
    ids, gates = ids_ref[...], gates_ref[...]
    hits, named = slot_matrix(experts, ids)
    for d in range(experts):
        chosen_ref[d * CAP : (d + 1) * CAP, :] = jnp.where(hits[d], 1.0, 0.0).astype(BF16)
    weight = jnp.where(ids[0:1, :] == named, gates[0:1, :], 0.0) + jnp.where(
        ids[1:2, :] == named, gates[1:2, :], 0.0
    )
    coarse = weight.astype(BF16).astype(F32)
    for ref, part in ((coarse_ref, coarse), (fine_ref, weight - coarse)):
        slots = [jnp.where(hits[d], part[d : d + 1, :], 0.0) for d in range(experts)]
        ref[...] = jnp.concatenate(slots, axis=0).T.astype(BF16)


def spread(experts, ids, gates):
    tokens = ids.shape[1]
    return pl.pallas_call(
        functools.partial(spread_kernel, experts),
        out_shape=[jax.ShapeDtypeStruct((tokens, experts * CAP), BF16)] * 2
        + [jax.ShapeDtypeStruct((experts * CAP, tokens), BF16)],
        in_specs=[VMEM] * 2,
        out_specs=[VMEM] * 3,
        compiler_params=params(16),
        cost_estimate=cost(0, 4 * tokens * experts * CAP),
        name="spread_gates",
    )(ids, gates)


def combine_kernel(groups, experts, chunks, coarse_ref, fine_ref, *rest):
    kept, blocks = rest[:chunks], rest[chunks : chunks + experts]
    out_ref, made_ref, sems = rest[chunks + experts :]
    width = kept[0].shape[1] // groups
    copies = []
    for g in range(groups):
        span = slice(g * chunks * width, (g + 1) * chunks * width)
        rows = jnp.concatenate([block[:, span] for block in blocks], axis=0)
        total = jnp.concatenate(
            [ref[:, g * width : (g + 1) * width] for ref in kept], axis=1
        ).astype(F32)
        total += jnp.dot(coarse_ref[...], rows, preferred_element_type=F32)
        total += jnp.dot(fine_ref[...], rows, preferred_element_type=F32)
        made_ref[:, span] = total.astype(BF16)
        copies.append(
            pltpu.make_async_copy(made_ref.at[:, span], out_ref.at[0, :, span], sems.at[g])
        )
        copies[-1].start()
    for copy in copies:
        copy.wait()


def combine(groups, weights, kept, blocks):
    tokens, features = weights[0].shape[0], blocks[0].shape[1]
    experts = len(blocks)
    return pl.pallas_call(
        functools.partial(combine_kernel, groups, experts, len(kept)),
        out_shape=jax.ShapeDtypeStruct((1, tokens, features), BF16),
        in_specs=[VMEM] * (2 + len(kept) + experts),
        out_specs=HBM,
        scratch_shapes=[
            pltpu.VMEM((tokens, features), BF16),
            pltpu.SemaphoreType.DMA((groups,)),
        ],
        compiler_params=params(24),
        cost_estimate=cost(4 * experts * CAP * tokens * features, 8 * tokens * features),
        name="combine",
    )(*weights, *kept, *blocks)


def after(values, *earlier):
    return lax.optimization_barrier((values, earlier))[0]


def local(
    query_rows, key_rows, value_rows, norm_gain, expert_ids, gate_weights, w_gate, w_up, w_down
):
    features = query_rows.shape[2]
    head_size = features // HEADS
    groups, experts = lax.axis_size("seq"), lax.axis_size("expert")
    per_group = HEADS // groups
    group_width = per_group * head_size
    chunks = CHUNKS if per_group % CHUNKS == 0 else 1
    width = group_width // chunks
    ids, gates = expert_ids[0].T, gate_weights[0].T
    gain = norm_gain.reshape(1, features)
    half = experts // 2
    middle = half + experts // 4

    def exchange(blocks, name):
        with jax.named_scope(name):
            return [blocks[0]] + [swap(blocks[d], "seq", d) for d in range(1, groups)]

    def send(block, distance, name):
        with jax.named_scope(f"{name}{distance}"):
            return swap(block, "expert", distance)

    first = [(d, 0) for d in range(1, groups)]
    others = [(0, 0)] + [(d, c) for c in range(1, chunks) for d in range(groups)]
    packed = pack(first, chunks, width, PACK_MIB, query_rows, key_rows, value_rows)
    own, *rest = pack(others, chunks, width, 8, query_rows, key_rows, value_rows)
    packed = [own, *packed, *rest]
    received = [
        exchange(packed[c * groups : (c + 1) * groups], f"qkv{c}_") for c in range(chunks)
    ]
    *weights, chosen = spread(experts, ids, gates)
    received[-1][0] = after(received[-1][0], weights)
    heads = [attend(width, head_size, received[c]) for c in range(chunks)]
    kept, arrived = [], [[] for _ in range(experts)]
    for c in range(chunks):
        last = c == chunks - 1
        out = heads[c]
        *rows, own = select(groups, experts, chosen, exchange(out, f"heads{c}_"), kept, last)
        kept.append(own)
        for d in range(half, middle):
            row = rows[d - half] if c == 0 else after(rows[d - half], arrived[d][-1])
            arrived[d].append(send(row, d, f"rows{c}_"))
    whole = rows[middle - half :]
    for d in range(middle, experts):
        arrived[d].append(send(whole[d - middle], d, "rows_"))
    whole = whole[experts - middle :]
    arrived[0].append(whole[0])
    for d in range(1, half):
        arrived[d].append(send(whole[d], d, "rows_"))
    returned = [None] * experts
    for members in (range(half, middle), range(middle, experts), range(half)):
        produced = run_experts(
            groups, chunks, width, gain, w_gate, w_up, w_down,
            [arrived[d] for d in members],
        )
        for d, block in zip(members, produced):
            returned[d] = block if d == 0 else send(block, d, "back_")
    return combine(groups, weights, kept, returned)


def solution(mesh):
    rows = P("expert", "seq", None)
    weights = P("expert", None, None)
    return jax.shard_map(
        local,
        mesh=mesh,
        in_specs=(rows, rows, rows, P(), rows, rows, weights, weights, weights),
        out_specs=rows,
        check_vma=False,
    )
```

```python
import functools
import math

import jax
import jax.numpy as jnp
from jax import lax
from jax.experimental import pallas as pl
from jax.experimental.pallas import tpu as pltpu
from jax.sharding import PartitionSpec as P

HEADS = 16
CAP = 32
CHUNKS = 2
PACK_MIB = 53
F32 = jnp.float32
BF16 = jnp.bfloat16
HBM = pl.BlockSpec(memory_space=pltpu.HBM)
VMEM = pl.BlockSpec(memory_space=pltpu.VMEM)


def swap(x, axis, distance):
    size = lax.axis_size(axis)
    return lax.ppermute(x, axis, [(i, i ^ distance) for i in range(size)])


def params(mib):
    return pltpu.CompilerParams(vmem_limit_bytes=mib << 20)


def cost(flops, moved):
    return pl.CostEstimate(flops=flops, bytes_accessed=moved, transcendentals=0)


def pack_kernel(places, chunks, width, q_ref, k_ref, v_ref, *rest):
    outs, sems = rest[:-1], rest[-1]
    me = lax.axis_index("seq")
    copies = []
    for out, (distance, c) in zip(outs, places):
        column = pl.multiple_of(((me ^ distance) * chunks + c) * width, 128)
        for i, ref in enumerate((q_ref, k_ref, v_ref)):
            copies.append(
                pltpu.make_async_copy(
                    ref.at[0, :, pl.ds(column, width)], out.at[i], sems.at[len(copies)]
                )
            )
    for copy in copies:
        copy.start()
    for copy in copies:
        copy.wait()


def pack(places, chunks, width, mib, q, k, v):
    tokens = q.shape[1]
    count = 3 * len(places)
    return pl.pallas_call(
        functools.partial(pack_kernel, places, chunks, width),
        out_shape=[jax.ShapeDtypeStruct((3, tokens, width), BF16)] * len(places),
        in_specs=[HBM] * 3,
        out_specs=[VMEM] * len(places),
        scratch_shapes=[pltpu.SemaphoreType.DMA((count,))],
        compiler_params=params(mib),
        cost_estimate=cost(0, 4 * count * tokens * width),
        name="pack_heads",
    )(q, k, v)


def attend_kernel(groups, width, head_size, *rest):
    blocks, outs = rest[:groups], rest[groups:]
    scale = head_size**-0.5 * math.log2(math.e)
    step = min(groups, 4)
    for head in range(width // head_size):
        lanes = slice(head * head_size, (head + 1) * head_size)
        keys = jnp.concatenate([block[1, :, lanes] for block in blocks], axis=0)
        values = jnp.concatenate([block[2, :, lanes] for block in blocks], axis=0)
        for first in range(0, groups, step):
            members = range(first, min(first + step, groups))
            scores = [
                lax.dot_general(
                    blocks[b][0, :, lanes], keys, (((1,), (1,)), ((), ())),
                    preferred_element_type=F32,
                )
                for b in members
            ]
            peaks = [jnp.max(part, axis=-1, keepdims=True) for part in scores]
            exponentials = [jnp.exp2((s - p) * scale) for s, p in zip(scores, peaks)]
            totals = [jnp.sum(part, axis=-1, keepdims=True) for part in exponentials]
            weighted = [
                jnp.dot(part.astype(BF16), values, preferred_element_type=F32)
                for part in exponentials
            ]
            for b, part, total in zip(members, weighted, totals):
                outs[b][:, lanes] = (part * (1.0 / total)).astype(BF16)


def attend(width, head_size, blocks):
    groups, tokens = len(blocks), blocks[0].shape[1]
    total = groups * tokens
    return pl.pallas_call(
        functools.partial(attend_kernel, groups, width, head_size),
        out_shape=[jax.ShapeDtypeStruct((tokens, width), BF16)] * groups,
        in_specs=[VMEM] * groups,
        out_specs=[VMEM] * groups,
        compiler_params=params(32),
        cost_estimate=cost(160 * total * total * width, 80 * total * width),
        name="attend",
    )(*blocks)


def slot_matrix(experts, ids):
    tokens = ids.shape[1]
    me = lax.axis_index("expert")
    named = lax.broadcasted_iota(jnp.int32, (experts, tokens), 0) ^ me
    matches = jnp.where((ids[0:1, :] == named) | (ids[1:2, :] == named), 1.0, 0.0)
    earlier = jnp.where(
        lax.broadcasted_iota(jnp.int32, (tokens, tokens), 0)
        < lax.broadcasted_iota(jnp.int32, (tokens, tokens), 1),
        1.0,
        0.0,
    )
    rank = jnp.dot(matches.astype(BF16), earlier.astype(BF16), preferred_element_type=F32)
    rank = jnp.where(matches > 0.0, rank, -1.0).astype(jnp.int32)
    slots = lax.broadcasted_iota(jnp.int32, (CAP, tokens), 0)
    return [slots == rank[d : d + 1, :] for d in range(experts)], named


def select_kernel(groups, experts, width, earlier, last, chosen_ref, *rest):
    blocks, before = rest[:groups], rest[groups : groups + earlier]
    half, middle = experts // 2, experts // 2 + experts // 4
    count = experts if last else middle - half
    outs = rest[groups + earlier : groups + earlier + count]
    kept = rest[groups + earlier + count]
    me = lax.axis_index("seq")
    for d in range(groups):
        column = pl.multiple_of((me ^ d) * width, 128)
        kept[:, pl.ds(column, width)] = blocks[d][...]

    def pick(low, high, rows, targets):
        picked = jnp.dot(
            chosen_ref[low * CAP : high * CAP], rows, preferred_element_type=F32
        ).astype(BF16)
        for i, target in enumerate(targets):
            target[...] = picked[i * CAP : (i + 1) * CAP]

    pick(half, middle, kept[...], outs[: middle - half])
    if last:
        parts = [ref[...] for ref in before] + [kept[...]]
        full = jnp.concatenate(parts, axis=1) if earlier else parts[0]
        pick(middle, experts, full, outs[middle - half : experts - half])
        pick(0, half, full, outs[experts - half :])


def select(groups, experts, chosen, blocks, before, last):
    tokens, width = blocks[0].shape
    part = groups * width
    whole = part * (len(before) + 1)
    quarter = experts // 4
    shapes = [(CAP, part)] * quarter
    if last:
        shapes += [(CAP, whole)] * (experts - quarter)
    shapes.append((tokens, part))
    return pl.pallas_call(
        functools.partial(select_kernel, groups, experts, width, len(before), last),
        out_shape=[jax.ShapeDtypeStruct(shape, BF16) for shape in shapes],
        in_specs=[VMEM] * (1 + groups + len(before)),
        out_specs=[VMEM] * len(shapes),
        compiler_params=params(16),
        cost_estimate=cost(2 * experts * CAP * tokens * part, 8 * tokens * part),
        name="select_rows",
    )(chosen, *blocks, *before)


def experts_kernel(groups, chunks, width, held, gain_ref, gate_ref, up_ref, down_ref, *rest):
    inputs, count = sum(held), len(held)
    blocks, outs = rest[:inputs], rest[inputs : inputs + count]
    rows_ref, hidden_ref = rest[inputs + count :]
    used = 0
    for i in range(count):
        mine = [blocks[k][...] for k in range(used, used + held[i])]
        used += held[i]
        row = jnp.concatenate(mine, axis=1) if len(mine) > 1 else mine[0]
        parts = []
        for g in range(groups):
            for c in range(chunks):
                first = (c * groups + g) * width
                parts.append(row[:, first : first + width].astype(F32))
        row = jnp.concatenate(parts, axis=1)
        scale = lax.rsqrt(jnp.mean(row * row, axis=-1, keepdims=True) + 1e-06)
        rows_ref[i * CAP : (i + 1) * CAP, :] = (row * scale * gain_ref[...]).astype(BF16)
    units, features = down_ref.shape[1:]
    tile = 256 if units % 256 == 0 else 128
    for first in range(0, units, tile):
        lanes = slice(first, first + tile)
        gate = jnp.dot(rows_ref[...], gate_ref[0, :, lanes], preferred_element_type=F32)
        up = jnp.dot(rows_ref[...], up_ref[0, :, lanes], preferred_element_type=F32)
        hidden_ref[:, lanes] = (gate / (1.0 + jnp.exp(-gate)) * up).astype(BF16)
    for first in range(0, features, 512):
        lanes = slice(first, first + 512)
        made = jnp.dot(hidden_ref[...], down_ref[0, :, lanes], preferred_element_type=F32)
        for i in range(count):
            outs[i][:, lanes] = made[i * CAP : (i + 1) * CAP].astype(BF16)


def run_experts(groups, chunks, width, gain, w_gate, w_up, w_down, blocks):
    held = tuple(len(block) for block in blocks)
    count = len(held)
    features, units = w_gate.shape[1:]
    flat = [part for block in blocks for part in block]
    return pl.pallas_call(
        functools.partial(experts_kernel, groups, chunks, width, held),
        out_shape=[jax.ShapeDtypeStruct((CAP, features), BF16)] * count,
        in_specs=[VMEM] * (4 + len(flat)),
        out_specs=[VMEM] * count,
        scratch_shapes=[
            pltpu.VMEM((count * CAP, features), BF16),
            pltpu.VMEM((count * CAP, units), BF16),
        ],
        compiler_params=params(24),
        cost_estimate=cost(count * CAP * features, features * units // 100),
        name="experts",
    )(gain, w_gate, w_up, w_down, *flat)


def spread_kernel(experts, ids_ref, gates_ref, weight_ref, chosen_ref):
    ids, gates = ids_ref[...], gates_ref[...]
    hits, named = slot_matrix(experts, ids)
    for d in range(experts):
        chosen_ref[d * CAP : (d + 1) * CAP, :] = jnp.where(hits[d], 1.0, 0.0).astype(BF16)
    weight = jnp.where(ids[0:1, :] == named, gates[0:1, :], 0.0) + jnp.where(
        ids[1:2, :] == named, gates[1:2, :], 0.0
    )
    slots = [jnp.where(hits[d], weight[d : d + 1, :], 0.0) for d in range(experts)]
    weight_ref[...] = jnp.concatenate(slots, axis=0).T.astype(BF16)


def spread(experts, ids, gates):
    tokens = ids.shape[1]
    return pl.pallas_call(
        functools.partial(spread_kernel, experts),
        out_shape=[
            jax.ShapeDtypeStruct((tokens, experts * CAP), BF16),
            jax.ShapeDtypeStruct((experts * CAP, tokens), BF16),
        ],
        in_specs=[VMEM] * 2,
        out_specs=[VMEM] * 2,
        compiler_params=params(16),
        cost_estimate=cost(0, 4 * tokens * experts * CAP),
        name="spread_gates",
    )(ids, gates)


def combine_kernel(groups, experts, chunks, weight_ref, *rest):
    kept, blocks = rest[:chunks], rest[chunks : chunks + experts]
    out_ref, made_ref, sems = rest[chunks + experts :]
    width = kept[0].shape[1] // groups
    copies = []
    for g in range(groups):
        span = slice(g * chunks * width, (g + 1) * chunks * width)
        rows = jnp.concatenate([block[:, span] for block in blocks], axis=0)
        total = jnp.concatenate(
            [ref[:, g * width : (g + 1) * width] for ref in kept], axis=1
        ).astype(F32)
        total += jnp.dot(weight_ref[...], rows, preferred_element_type=F32)
        made_ref[:, span] = total.astype(BF16)
        copies.append(
            pltpu.make_async_copy(made_ref.at[:, span], out_ref.at[0, :, span], sems.at[g])
        )
        copies[-1].start()
    for copy in copies:
        copy.wait()


def combine(groups, weights, kept, blocks):
    tokens, features = weights.shape[0], blocks[0].shape[1]
    experts = len(blocks)
    return pl.pallas_call(
        functools.partial(combine_kernel, groups, experts, len(kept)),
        out_shape=jax.ShapeDtypeStruct((1, tokens, features), BF16),
        in_specs=[VMEM] * (1 + len(kept) + experts),
        out_specs=HBM,
        scratch_shapes=[
            pltpu.VMEM((tokens, features), BF16),
            pltpu.SemaphoreType.DMA((groups,)),
        ],
        compiler_params=params(24),
        cost_estimate=cost(4 * experts * CAP * tokens * features, 8 * tokens * features),
        name="combine",
    )(weights, *kept, *blocks)


def after(values, *earlier):
    return lax.optimization_barrier((values, earlier))[0]


def local(
    query_rows, key_rows, value_rows, norm_gain, expert_ids, gate_weights, w_gate, w_up, w_down
):
    features = query_rows.shape[2]
    head_size = features // HEADS
    groups, experts = lax.axis_size("seq"), lax.axis_size("expert")
    per_group = HEADS // groups
    group_width = per_group * head_size
    chunks = CHUNKS if per_group % CHUNKS == 0 else 1
    width = group_width // chunks
    ids, gates = expert_ids[0].T, gate_weights[0].T
    gain = norm_gain.reshape(1, features)
    half = experts // 2
    middle = half + experts // 4

    def exchange(blocks, name):
        with jax.named_scope(name):
            return [blocks[0]] + [swap(blocks[d], "seq", d) for d in range(1, groups)]

    def send(block, distance, name):
        with jax.named_scope(f"{name}{distance}"):
            return swap(block, "expert", distance)

    first = [(d, 0) for d in range(1, groups)]
    others = [(0, 0)] + [(d, c) for c in range(1, chunks) for d in range(groups)]
    packed = pack(first, chunks, width, PACK_MIB, query_rows, key_rows, value_rows)
    own, *rest = pack(others, chunks, width, 8, query_rows, key_rows, value_rows)
    packed = [own, *packed, *rest]
    received = [
        exchange(packed[c * groups : (c + 1) * groups], f"qkv{c}_") for c in range(chunks)
    ]
    weights, chosen = spread(experts, ids, gates)
    received[-1][0] = after(received[-1][0], weights)
    heads = [attend(width, head_size, received[c]) for c in range(chunks)]
    kept, arrived = [], [[] for _ in range(experts)]
    for c in range(chunks):
        last = c == chunks - 1
        out = heads[c]
        *rows, own = select(groups, experts, chosen, exchange(out, f"heads{c}_"), kept, last)
        kept.append(own)
        for d in range(half, middle):
            row = rows[d - half] if c == 0 else after(rows[d - half], arrived[d][-1])
            arrived[d].append(send(row, d, f"rows{c}_"))
    whole = rows[middle - half :]
    for d in range(middle, experts):
        arrived[d].append(send(whole[d - middle], d, "rows_"))
    whole = whole[experts - middle :]
    arrived[0].append(whole[0])
    for d in range(1, half):
        arrived[d].append(send(whole[d], d, "rows_"))
    returned = [None] * experts
    for members in (range(half, middle), range(middle, experts), range(half)):
        produced = run_experts(
            groups, chunks, width, gain, w_gate, w_up, w_down,
            [arrived[d] for d in members],
        )
        for d, block in zip(members, produced):
            returned[d] = block if d == 0 else send(block, d, "back_")
    return combine(groups, weights, kept, returned)


def solution(mesh):
    rows = P("expert", "seq", None)
    weights = P("expert", None, None)
    return jax.shard_map(
        local,
        mesh=mesh,
        in_specs=(rows, rows, rows, P(), rows, rows, weights, weights, weights),
        out_specs=rows,
        check_vma=False,
    )
```

```python
import functools
import math

import jax
import jax.numpy as jnp
from jax import lax
from jax.experimental import pallas as pl
from jax.experimental.pallas import tpu as pltpu
from jax.sharding import PartitionSpec as P

HEADS = 16
CAP = 32
CHUNKS = 2
PACK_MIB = 53
F32 = jnp.float32
BF16 = jnp.bfloat16
HBM = pl.BlockSpec(memory_space=pltpu.HBM)
VMEM = pl.BlockSpec(memory_space=pltpu.VMEM)


def swap(x, axis, distance):
    size = lax.axis_size(axis)
    return lax.ppermute(x, axis, [(i, i ^ distance) for i in range(size)])


def params(mib):
    return pltpu.CompilerParams(vmem_limit_bytes=mib << 20)


def cost(flops, moved):
    return pl.CostEstimate(flops=flops, bytes_accessed=moved, transcendentals=0)


def pack_kernel(places, chunks, width, q_ref, k_ref, v_ref, *rest):
    outs, sems = rest[:-1], rest[-1]
    me = lax.axis_index("seq")
    copies = []
    for out, (distance, c) in zip(outs, places):
        column = pl.multiple_of(((me ^ distance) * chunks + c) * width, 128)
        for i, ref in enumerate((q_ref, k_ref, v_ref)):
            copies.append(
                pltpu.make_async_copy(
                    ref.at[0, :, pl.ds(column, width)], out.at[i], sems.at[len(copies)]
                )
            )
    for copy in copies:
        copy.start()
    for copy in copies:
        copy.wait()


def pack(places, chunks, width, mib, q, k, v):
    tokens = q.shape[1]
    count = 3 * len(places)
    return pl.pallas_call(
        functools.partial(pack_kernel, places, chunks, width),
        out_shape=[jax.ShapeDtypeStruct((3, tokens, width), BF16)] * len(places),
        in_specs=[HBM] * 3,
        out_specs=[VMEM] * len(places),
        scratch_shapes=[pltpu.SemaphoreType.DMA((count,))],
        compiler_params=params(mib),
        cost_estimate=cost(0, 4 * count * tokens * width),
        name="pack_heads",
    )(q, k, v)


def attend_kernel(groups, width, head_size, *rest):
    blocks, outs = rest[:groups], rest[groups:]
    scale = head_size**-0.5 * math.log2(math.e)
    step = min(groups, 4)
    for head in range(width // head_size):
        lanes = slice(head * head_size, (head + 1) * head_size)
        keys = jnp.concatenate([block[1, :, lanes] for block in blocks], axis=0)
        values = jnp.concatenate([block[2, :, lanes] for block in blocks], axis=0)
        for first in range(0, groups, step):
            members = range(first, min(first + step, groups))
            scores = [
                lax.dot_general(
                    blocks[b][0, :, lanes], keys, (((1,), (1,)), ((), ())),
                    preferred_element_type=F32,
                )
                for b in members
            ]
            peaks = [jnp.max(part, axis=-1, keepdims=True) for part in scores]
            exponentials = [jnp.exp2((s - p) * scale) for s, p in zip(scores, peaks)]
            totals = [jnp.sum(part, axis=-1, keepdims=True) for part in exponentials]
            weighted = [
                jnp.dot(part.astype(BF16), values, preferred_element_type=F32)
                for part in exponentials
            ]
            for b, part, total in zip(members, weighted, totals):
                outs[b][:, lanes] = (part * (1.0 / total)).astype(BF16)


def attend(width, head_size, blocks):
    groups, tokens = len(blocks), blocks[0].shape[1]
    total = groups * tokens
    return pl.pallas_call(
        functools.partial(attend_kernel, groups, width, head_size),
        out_shape=[jax.ShapeDtypeStruct((tokens, width), BF16)] * groups,
        in_specs=[VMEM] * groups,
        out_specs=[VMEM] * groups,
        compiler_params=params(32),
        cost_estimate=cost(160 * total * total * width, 80 * total * width),
        name="attend",
    )(*blocks)


def slot_matrix(experts, ids):
    tokens = ids.shape[1]
    me = lax.axis_index("expert")
    named = lax.broadcasted_iota(jnp.int32, (experts, tokens), 0) ^ me
    matches = jnp.where((ids[0:1, :] == named) | (ids[1:2, :] == named), 1.0, 0.0)
    earlier = jnp.where(
        lax.broadcasted_iota(jnp.int32, (tokens, tokens), 0)
        < lax.broadcasted_iota(jnp.int32, (tokens, tokens), 1),
        1.0,
        0.0,
    )
    rank = jnp.dot(matches.astype(BF16), earlier.astype(BF16), preferred_element_type=F32)
    rank = jnp.where(matches > 0.0, rank, -1.0).astype(jnp.int32)
    slots = lax.broadcasted_iota(jnp.int32, (CAP, tokens), 0)
    return [slots == rank[d : d + 1, :] for d in range(experts)], named


def select_kernel(groups, experts, width, earlier, last, chosen_ref, *rest):
    blocks, before = rest[:groups], rest[groups : groups + earlier]
    half, middle = experts // 2, experts // 2 + experts // 4
    count = experts if last else middle - half
    outs = rest[groups + earlier : groups + earlier + count]
    kept = rest[groups + earlier + count]
    me = lax.axis_index("seq")
    for d in range(groups):
        column = pl.multiple_of((me ^ d) * width, 128)
        kept[:, pl.ds(column, width)] = blocks[d][...]

    def pick(low, high, rows, targets):
        picked = jnp.dot(
            chosen_ref[low * CAP : high * CAP], rows, preferred_element_type=F32
        ).astype(BF16)
        for i, target in enumerate(targets):
            target[...] = picked[i * CAP : (i + 1) * CAP]

    pick(half, middle, kept[...], outs[: middle - half])
    if last:
        parts = [ref[...] for ref in before] + [kept[...]]
        full = jnp.concatenate(parts, axis=1) if earlier else parts[0]
        pick(middle, experts, full, outs[middle - half : experts - half])
        pick(0, half, full, outs[experts - half :])


def select(groups, experts, chosen, blocks, before, last):
    tokens, width = blocks[0].shape
    part = groups * width
    whole = part * (len(before) + 1)
    quarter = experts // 4
    shapes = [(CAP, part)] * quarter
    if last:
        shapes += [(CAP, whole)] * (experts - quarter)
    shapes.append((tokens, part))
    return pl.pallas_call(
        functools.partial(select_kernel, groups, experts, width, len(before), last),
        out_shape=[jax.ShapeDtypeStruct(shape, BF16) for shape in shapes],
        in_specs=[VMEM] * (1 + groups + len(before)),
        out_specs=[VMEM] * len(shapes),
        compiler_params=params(16),
        cost_estimate=cost(2 * experts * CAP * tokens * part, 8 * tokens * part),
        name="select_rows",
    )(chosen, *blocks, *before)


def experts_kernel(groups, chunks, width, held, gain_ref, gate_ref, up_ref, down_ref, *rest):
    inputs, count = sum(held), len(held)
    blocks, outs = rest[:inputs], rest[inputs : inputs + count]
    rows_ref, hidden_ref = rest[inputs + count :]
    used = 0
    for i in range(count):
        mine = [blocks[k][...] for k in range(used, used + held[i])]
        used += held[i]
        row = jnp.concatenate(mine, axis=1) if len(mine) > 1 else mine[0]
        parts = []
        for g in range(groups):
            for c in range(chunks):
                first = (c * groups + g) * width
                parts.append(row[:, first : first + width].astype(F32))
        row = jnp.concatenate(parts, axis=1)
        scale = lax.rsqrt(jnp.mean(row * row, axis=-1, keepdims=True) + 1e-06)
        rows_ref[i * CAP : (i + 1) * CAP, :] = (row * scale * gain_ref[...]).astype(BF16)
    units, features = down_ref.shape[1:]
    tile = 256 if units % 256 == 0 else 128
    for first in range(0, units, tile):
        lanes = slice(first, first + tile)
        gate = jnp.dot(rows_ref[...], gate_ref[0, :, lanes], preferred_element_type=F32)
        up = jnp.dot(rows_ref[...], up_ref[0, :, lanes], preferred_element_type=F32)
        hidden_ref[:, lanes] = (gate / (1.0 + jnp.exp(-gate)) * up).astype(BF16)
    for first in range(0, features, 512):
        lanes = slice(first, first + 512)
        made = jnp.dot(hidden_ref[...], down_ref[0, :, lanes], preferred_element_type=F32)
        for i in range(count):
            outs[i][:, lanes] = made[i * CAP : (i + 1) * CAP].astype(BF16)


def run_experts(groups, chunks, width, gain, w_gate, w_up, w_down, blocks):
    held = tuple(len(block) for block in blocks)
    count = len(held)
    features, units = w_gate.shape[1:]
    flat = [part for block in blocks for part in block]
    return pl.pallas_call(
        functools.partial(experts_kernel, groups, chunks, width, held),
        out_shape=[jax.ShapeDtypeStruct((CAP, features), BF16)] * count,
        in_specs=[VMEM] * (4 + len(flat)),
        out_specs=[VMEM] * count,
        scratch_shapes=[
            pltpu.VMEM((count * CAP, features), BF16),
            pltpu.VMEM((count * CAP, units), BF16),
        ],
        compiler_params=params(24),
        cost_estimate=cost(count * CAP * features, features * units // 100),
        name="experts",
    )(gain, w_gate, w_up, w_down, *flat)


def spread_kernel(experts, ids_ref, gates_ref, weight_ref, chosen_ref):
    ids, gates = ids_ref[...], gates_ref[...]
    hits, named = slot_matrix(experts, ids)
    for d in range(experts):
        chosen_ref[d * CAP : (d + 1) * CAP, :] = jnp.where(hits[d], 1.0, 0.0).astype(BF16)
    weight = jnp.where(ids[0:1, :] == named, gates[0:1, :], 0.0) + jnp.where(
        ids[1:2, :] == named, gates[1:2, :], 0.0
    )
    slots = [jnp.where(hits[d], weight[d : d + 1, :], 0.0) for d in range(experts)]
    weight_ref[...] = jnp.concatenate(slots, axis=0).T.astype(BF16)


def spread(experts, ids, gates):
    tokens = ids.shape[1]
    return pl.pallas_call(
        functools.partial(spread_kernel, experts),
        out_shape=[
            jax.ShapeDtypeStruct((tokens, experts * CAP), BF16),
            jax.ShapeDtypeStruct((experts * CAP, tokens), BF16),
        ],
        in_specs=[VMEM] * 2,
        out_specs=[VMEM] * 2,
        compiler_params=params(16),
        cost_estimate=cost(0, 4 * tokens * experts * CAP),
        name="spread_gates",
    )(ids, gates)


def combine_kernel(groups, experts, chunks, weight_ref, *rest):
    kept, blocks = rest[:chunks], rest[chunks : chunks + experts]
    out_ref, made_ref, sems = rest[chunks + experts :]
    width = kept[0].shape[1] // groups
    copies = []
    for g in range(groups):
        span = slice(g * chunks * width, (g + 1) * chunks * width)
        rows = jnp.concatenate([block[:, span] for block in blocks], axis=0)
        total = jnp.concatenate(
            [ref[:, g * width : (g + 1) * width] for ref in kept], axis=1
        ).astype(F32)
        total += jnp.dot(weight_ref[...], rows, preferred_element_type=F32)
        made_ref[:, span] = total.astype(BF16)
        copies.append(
            pltpu.make_async_copy(made_ref.at[:, span], out_ref.at[0, :, span], sems.at[g])
        )
        copies[-1].start()
    for copy in copies:
        copy.wait()


def combine(groups, weights, kept, blocks):
    tokens, features = weights.shape[0], blocks[0].shape[1]
    experts = len(blocks)
    return pl.pallas_call(
        functools.partial(combine_kernel, groups, experts, len(kept)),
        out_shape=jax.ShapeDtypeStruct((1, tokens, features), BF16),
        in_specs=[VMEM] * (1 + len(kept) + experts),
        out_specs=HBM,
        scratch_shapes=[
            pltpu.VMEM((tokens, features), BF16),
            pltpu.SemaphoreType.DMA((groups,)),
        ],
        compiler_params=params(24),
        cost_estimate=cost(4 * experts * CAP * tokens * features, 8 * tokens * features),
        name="combine",
    )(weights, *kept, *blocks)


def after(values, *earlier):
    return lax.optimization_barrier((values, earlier))[0]


def local(
    query_rows, key_rows, value_rows, norm_gain, expert_ids, gate_weights, w_gate, w_up, w_down
):
    features = query_rows.shape[2]
    head_size = features // HEADS
    groups, experts = lax.axis_size("seq"), lax.axis_size("expert")
    per_group = HEADS // groups
    group_width = per_group * head_size
    chunks = CHUNKS if per_group % CHUNKS == 0 else 1
    width = group_width // chunks
    ids, gates = expert_ids[0].T, gate_weights[0].T
    gain = norm_gain.reshape(1, features)
    half = experts // 2
    middle = half + experts // 4

    def exchange(blocks, name):
        with jax.named_scope(name):
            return [blocks[0]] + [swap(blocks[d], "seq", d) for d in range(1, groups)]

    def send(block, distance, name):
        with jax.named_scope(f"{name}{distance}"):
            return swap(block, "expert", distance)

    first = [(d, 0) for d in range(1, groups)]
    others = [(0, 0)] + [(d, c) for c in range(1, chunks) for d in range(groups)]
    packed = pack(first, chunks, width, PACK_MIB, query_rows, key_rows, value_rows)
    own, *rest = pack(others, chunks, width, 8, query_rows, key_rows, value_rows)
    packed = [own, *packed, *rest]
    received = [
        exchange(packed[c * groups : (c + 1) * groups], f"qkv{c}_") for c in range(chunks)
    ]
    weights, chosen = spread(experts, ids, gates)
    received[-1][0] = after(received[-1][0], weights)
    heads = [attend(width, head_size, received[c]) for c in range(chunks)]
    kept, arrived = [], [[] for _ in range(experts)]
    for c in range(chunks):
        last = c == chunks - 1
        out = heads[c] if c == 0 else [*heads[c][:-1], after(heads[c][-1], kept[-1])]
        *rows, own = select(groups, experts, chosen, exchange(out, f"heads{c}_"), kept, last)
        kept.append(own)
        for d in range(half, middle):
            row = rows[d - half] if c == 0 else after(rows[d - half], arrived[d][-1])
            arrived[d].append(send(row, d, f"rows{c}_"))
    whole = rows[middle - half :]
    for d in range(middle, experts):
        arrived[d].append(send(whole[d - middle], d, "rows_"))
    whole = whole[experts - middle :]
    arrived[0].append(whole[0])
    for d in range(1, half):
        arrived[d].append(send(whole[d], d, "rows_"))
    returned = [None] * experts
    for members in (range(half, middle), range(middle, experts), range(half)):
        produced = run_experts(
            groups, chunks, width, gain, w_gate, w_up, w_down,
            [arrived[d] for d in members],
        )
        for d, block in zip(members, produced):
            returned[d] = block if d == 0 else send(block, d, "back_")
    return combine(groups, weights, kept, returned)


def solution(mesh):
    rows = P("expert", "seq", None)
    weights = P("expert", None, None)
    return jax.shard_map(
        local,
        mesh=mesh,
        in_specs=(rows, rows, rows, P(), rows, rows, weights, weights, weights),
        out_specs=rows,
        check_vma=False,
    )
```

```python
import functools
import math

import jax
import jax.numpy as jnp
from jax import lax
from jax.experimental import pallas as pl
from jax.experimental.pallas import tpu as pltpu
from jax.sharding import PartitionSpec as P

HEADS = 16
CAP = 32
CHUNKS = 2
PACK_MIB = 53
F32 = jnp.float32
BF16 = jnp.bfloat16
HBM = pl.BlockSpec(memory_space=pltpu.HBM)
VMEM = pl.BlockSpec(memory_space=pltpu.VMEM)


def swap(x, axis, distance):
    size = lax.axis_size(axis)
    return lax.ppermute(x, axis, [(i, i ^ distance) for i in range(size)])


def params(mib):
    return pltpu.CompilerParams(vmem_limit_bytes=mib << 20)


def cost(flops, moved):
    return pl.CostEstimate(flops=flops, bytes_accessed=moved, transcendentals=0)


def pack_kernel(places, chunks, width, q_ref, k_ref, v_ref, *rest):
    outs, sems = rest[:-1], rest[-1]
    me = lax.axis_index("seq")
    copies = []
    for out, (distance, c) in zip(outs, places):
        column = pl.multiple_of(((me ^ distance) * chunks + c) * width, 128)
        for i, ref in enumerate((q_ref, k_ref, v_ref)):
            copies.append(
                pltpu.make_async_copy(
                    ref.at[0, :, pl.ds(column, width)], out.at[i], sems.at[len(copies)]
                )
            )
    for copy in copies:
        copy.start()
    for copy in copies:
        copy.wait()


def pack(places, chunks, width, mib, q, k, v):
    tokens = q.shape[1]
    count = 3 * len(places)
    return pl.pallas_call(
        functools.partial(pack_kernel, places, chunks, width),
        out_shape=[jax.ShapeDtypeStruct((3, tokens, width), BF16)] * len(places),
        in_specs=[HBM] * 3,
        out_specs=[VMEM] * len(places),
        scratch_shapes=[pltpu.SemaphoreType.DMA((count,))],
        compiler_params=params(mib),
        cost_estimate=cost(0, 4 * count * tokens * width),
        name="pack_heads",
    )(q, k, v)


def attend_kernel(groups, width, head_size, *rest):
    blocks, outs = rest[:groups], rest[groups:]
    scale = head_size**-0.5 * math.log2(math.e)
    step = min(groups, 4)
    for head in range(width // head_size):
        lanes = slice(head * head_size, (head + 1) * head_size)
        keys = jnp.concatenate([block[1, :, lanes] for block in blocks], axis=0)
        values = jnp.concatenate([block[2, :, lanes] for block in blocks], axis=0)
        for first in range(0, groups, step):
            members = range(first, min(first + step, groups))
            scores = [
                lax.dot_general(
                    blocks[b][0, :, lanes], keys, (((1,), (1,)), ((), ())),
                    preferred_element_type=F32,
                )
                for b in members
            ]
            peaks = [jnp.max(part, axis=-1, keepdims=True) for part in scores]
            exponentials = [jnp.exp2((s - p) * scale) for s, p in zip(scores, peaks)]
            totals = [jnp.sum(part, axis=-1, keepdims=True) for part in exponentials]
            weighted = [
                jnp.dot(part.astype(BF16), values, preferred_element_type=F32)
                for part in exponentials
            ]
            for b, part, total in zip(members, weighted, totals):
                outs[b][:, lanes] = (part * (1.0 / total)).astype(BF16)


def attend(width, head_size, blocks):
    groups, tokens = len(blocks), blocks[0].shape[1]
    total = groups * tokens
    return pl.pallas_call(
        functools.partial(attend_kernel, groups, width, head_size),
        out_shape=[jax.ShapeDtypeStruct((tokens, width), BF16)] * groups,
        in_specs=[VMEM] * groups,
        out_specs=[VMEM] * groups,
        compiler_params=params(32),
        cost_estimate=cost(160 * total * total * width, 80 * total * width),
        name="attend",
    )(*blocks)


def slot_matrix(experts, ids):
    tokens = ids.shape[1]
    me = lax.axis_index("expert")
    named = lax.broadcasted_iota(jnp.int32, (experts, tokens), 0) ^ me
    matches = jnp.where((ids[0:1, :] == named) | (ids[1:2, :] == named), 1.0, 0.0)
    earlier = jnp.where(
        lax.broadcasted_iota(jnp.int32, (tokens, tokens), 0)
        < lax.broadcasted_iota(jnp.int32, (tokens, tokens), 1),
        1.0,
        0.0,
    )
    rank = jnp.dot(matches.astype(BF16), earlier.astype(BF16), preferred_element_type=F32)
    rank = jnp.where(matches > 0.0, rank, -1.0).astype(jnp.int32)
    slots = lax.broadcasted_iota(jnp.int32, (CAP, tokens), 0)
    return [slots == rank[d : d + 1, :] for d in range(experts)], named


def select_kernel(groups, experts, width, earlier, last, chosen_ref, *rest):
    blocks, before = rest[:groups], rest[groups : groups + earlier]
    half, middle = experts // 2, experts // 2 + experts // 4
    count = experts if last else middle - half
    outs = rest[groups + earlier : groups + earlier + count]
    kept = rest[groups + earlier + count]
    me = lax.axis_index("seq")
    for d in range(groups):
        column = pl.multiple_of((me ^ d) * width, 128)
        kept[:, pl.ds(column, width)] = blocks[d][...]

    def pick(low, high, rows, targets):
        picked = jnp.dot(
            chosen_ref[low * CAP : high * CAP], rows, preferred_element_type=F32
        ).astype(BF16)
        for i, target in enumerate(targets):
            target[...] = picked[i * CAP : (i + 1) * CAP]

    pick(half, middle, kept[...], outs[: middle - half])
    if last:
        parts = [ref[...] for ref in before] + [kept[...]]
        full = jnp.concatenate(parts, axis=1) if earlier else parts[0]
        pick(middle, experts, full, outs[middle - half : experts - half])
        pick(0, half, full, outs[experts - half :])


def select(groups, experts, chosen, blocks, before, last):
    tokens, width = blocks[0].shape
    part = groups * width
    whole = part * (len(before) + 1)
    quarter = experts // 4
    shapes = [(CAP, part)] * quarter
    if last:
        shapes += [(CAP, whole)] * (experts - quarter)
    shapes.append((tokens, part))
    return pl.pallas_call(
        functools.partial(select_kernel, groups, experts, width, len(before), last),
        out_shape=[jax.ShapeDtypeStruct(shape, BF16) for shape in shapes],
        in_specs=[VMEM] * (1 + groups + len(before)),
        out_specs=[VMEM] * len(shapes),
        compiler_params=params(16),
        cost_estimate=cost(2 * experts * CAP * tokens * part, 8 * tokens * part),
        name="select_rows",
    )(chosen, *blocks, *before)


def experts_kernel(groups, chunks, width, held, gain_ref, gate_ref, up_ref, down_ref, *rest):
    inputs, count = sum(held), len(held)
    blocks, outs = rest[:inputs], rest[inputs : inputs + count]
    rows_ref, hidden_ref = rest[inputs + count :]
    used = 0
    for i in range(count):
        mine = [blocks[k][...] for k in range(used, used + held[i])]
        used += held[i]
        row = jnp.concatenate(mine, axis=1) if len(mine) > 1 else mine[0]
        parts = []
        for g in range(groups):
            for c in range(chunks):
                first = (c * groups + g) * width
                parts.append(row[:, first : first + width].astype(F32))
        row = jnp.concatenate(parts, axis=1)
        scale = lax.rsqrt(jnp.mean(row * row, axis=-1, keepdims=True) + 1e-06)
        rows_ref[i * CAP : (i + 1) * CAP, :] = (row * scale * gain_ref[...]).astype(BF16)
    units, features = down_ref.shape[1:]
    tile = 256 if units % 256 == 0 else 128
    for first in range(0, units, tile):
        lanes = slice(first, first + tile)
        gate = jnp.dot(rows_ref[...], gate_ref[0, :, lanes], preferred_element_type=F32)
        up = jnp.dot(rows_ref[...], up_ref[0, :, lanes], preferred_element_type=F32)
        hidden_ref[:, lanes] = (gate / (1.0 + jnp.exp(-gate)) * up).astype(BF16)
    for first in range(0, features, 512):
        lanes = slice(first, first + 512)
        made = jnp.dot(hidden_ref[...], down_ref[0, :, lanes], preferred_element_type=F32)
        for i in range(count):
            outs[i][:, lanes] = made[i * CAP : (i + 1) * CAP].astype(BF16)


def run_experts(groups, chunks, width, gain, w_gate, w_up, w_down, blocks):
    held = tuple(len(block) for block in blocks)
    count = len(held)
    features, units = w_gate.shape[1:]
    flat = [part for block in blocks for part in block]
    return pl.pallas_call(
        functools.partial(experts_kernel, groups, chunks, width, held),
        out_shape=[jax.ShapeDtypeStruct((CAP, features), BF16)] * count,
        in_specs=[VMEM] * (4 + len(flat)),
        out_specs=[VMEM] * count,
        scratch_shapes=[
            pltpu.VMEM((count * CAP, features), BF16),
            pltpu.VMEM((count * CAP, units), BF16),
        ],
        compiler_params=params(24),
        cost_estimate=cost(count * CAP * features, features * units // 100),
        name="experts",
    )(gain, w_gate, w_up, w_down, *flat)


def spread_kernel(experts, ids_ref, gates_ref, weight_ref, chosen_ref):
    ids, gates = ids_ref[...], gates_ref[...]
    hits, named = slot_matrix(experts, ids)
    for d in range(experts):
        chosen_ref[d * CAP : (d + 1) * CAP, :] = jnp.where(hits[d], 1.0, 0.0).astype(BF16)
    weight = jnp.where(ids[0:1, :] == named, gates[0:1, :], 0.0) + jnp.where(
        ids[1:2, :] == named, gates[1:2, :], 0.0
    )
    slots = [jnp.where(hits[d], weight[d : d + 1, :], 0.0) for d in range(experts)]
    weight_ref[...] = jnp.concatenate(slots, axis=0).T.astype(BF16)


def spread(experts, ids, gates):
    tokens = ids.shape[1]
    return pl.pallas_call(
        functools.partial(spread_kernel, experts),
        out_shape=[
            jax.ShapeDtypeStruct((tokens, experts * CAP), BF16),
            jax.ShapeDtypeStruct((experts * CAP, tokens), BF16),
        ],
        in_specs=[VMEM] * 2,
        out_specs=[VMEM] * 2,
        compiler_params=params(16),
        cost_estimate=cost(0, 4 * tokens * experts * CAP),
        name="spread_gates",
    )(ids, gates)


def combine_kernel(groups, experts, chunks, weight_ref, *rest):
    kept, blocks = rest[:chunks], rest[chunks : chunks + experts]
    out_ref, made_ref, sems = rest[chunks + experts :]
    width = kept[0].shape[1] // groups
    step = 2 if groups % 2 == 0 else 1
    copies = []
    for first in range(0, groups, step):
        members = range(first, first + step)
        span = slice(first * chunks * width, (first + step) * chunks * width)
        rows = jnp.concatenate([block[:, span] for block in blocks], axis=0)
        total = jnp.concatenate(
            [ref[:, g * width : (g + 1) * width] for g in members for ref in kept], axis=1
        ).astype(F32)
        total += jnp.dot(weight_ref[...], rows, preferred_element_type=F32)
        made_ref[:, span] = total.astype(BF16)
        copies.append(
            pltpu.make_async_copy(made_ref.at[:, span], out_ref.at[0, :, span], sems.at[first])
        )
        copies[-1].start()
    for copy in copies:
        copy.wait()


def combine(groups, weights, kept, blocks):
    tokens, features = weights.shape[0], blocks[0].shape[1]
    experts = len(blocks)
    return pl.pallas_call(
        functools.partial(combine_kernel, groups, experts, len(kept)),
        out_shape=jax.ShapeDtypeStruct((1, tokens, features), BF16),
        in_specs=[VMEM] * (1 + len(kept) + experts),
        out_specs=HBM,
        scratch_shapes=[
            pltpu.VMEM((tokens, features), BF16),
            pltpu.SemaphoreType.DMA((groups,)),
        ],
        compiler_params=params(24),
        cost_estimate=cost(4 * experts * CAP * tokens * features, 8 * tokens * features),
        name="combine",
    )(weights, *kept, *blocks)


def after(values, *earlier):
    return lax.optimization_barrier((values, earlier))[0]


def local(
    query_rows, key_rows, value_rows, norm_gain, expert_ids, gate_weights, w_gate, w_up, w_down
):
    features = query_rows.shape[2]
    head_size = features // HEADS
    groups, experts = lax.axis_size("seq"), lax.axis_size("expert")
    per_group = HEADS // groups
    group_width = per_group * head_size
    chunks = CHUNKS if per_group % CHUNKS == 0 else 1
    width = group_width // chunks
    ids, gates = expert_ids[0].T, gate_weights[0].T
    gain = norm_gain.reshape(1, features)
    half = experts // 2
    middle = half + experts // 4

    def exchange(blocks, name):
        with jax.named_scope(name):
            return [blocks[0]] + [swap(blocks[d], "seq", d) for d in range(1, groups)]

    def send(block, distance, name):
        with jax.named_scope(f"{name}{distance}"):
            return swap(block, "expert", distance)

    first = [(d, 0) for d in range(1, groups)]
    others = [(0, 0)] + [(d, c) for c in range(1, chunks) for d in range(groups)]
    packed = pack(first, chunks, width, PACK_MIB, query_rows, key_rows, value_rows)
    own, *rest = pack(others, chunks, width, 8, query_rows, key_rows, value_rows)
    packed = [own, *packed, *rest]
    received = [
        exchange(packed[c * groups : (c + 1) * groups], f"qkv{c}_") for c in range(chunks)
    ]
    weights, chosen = spread(experts, ids, gates)
    received[-1][0] = after(received[-1][0], weights)
    heads = [attend(width, head_size, received[c]) for c in range(chunks)]
    kept, arrived = [], [[] for _ in range(experts)]
    for c in range(chunks):
        last = c == chunks - 1
        out = heads[c]
        *rows, own = select(groups, experts, chosen, exchange(out, f"heads{c}_"), kept, last)
        kept.append(own)
        for d in range(half, middle):
            row = rows[d - half] if c == 0 else after(rows[d - half], arrived[d][-1])
            arrived[d].append(send(row, d, f"rows{c}_"))
    whole = rows[middle - half :]
    for d in range(middle, experts):
        arrived[d].append(send(whole[d - middle], d, "rows_"))
    whole = whole[experts - middle :]
    arrived[0].append(whole[0])
    for d in range(1, half):
        arrived[d].append(send(whole[d], d, "rows_"))
    returned = [None] * experts
    for members in (range(half, middle), range(middle, experts), range(half)):
        produced = run_experts(
            groups, chunks, width, gain, w_gate, w_up, w_down,
            [arrived[d] for d in members],
        )
        for d, block in zip(members, produced):
            returned[d] = block if d == 0 else send(block, d, "back_")
    return combine(groups, weights, kept, returned)


def solution(mesh):
    rows = P("expert", "seq", None)
    weights = P("expert", None, None)
    return jax.shard_map(
        local,
        mesh=mesh,
        in_specs=(rows, rows, rows, P(), rows, rows, weights, weights, weights),
        out_specs=rows,
        check_vma=False,
    )
```
